256 devices in a mesh: queue: 64 (over y, z_hi, x), head: 4 (over z_lo, core).
Axes of the slice: x: 4, y: 4, z: 8 (z_hi: 4, z_lo: 2; z = z_hi * 2 + z_lo), core: 2. Of those that a mesh axis runs over, the one named last changes fastest.
Arguments:
- latents: bfloat16 [64, 512, 3072], P('queue', 'head'), may hold values from -6 to 6
- new_frame: bfloat16 [512, 3072], P('head'), may hold values from -6 to 6
- level_index: int32 [64], P('queue'), may hold values from 0 to 31, as said below
- window_offsets: int32 [64, 2], P('queue'), may hold values from 0 to 2
- mod_table: float32 [32, 3, 3072], replicated, may hold values from -3 to 3
- step_sizes: float32 [32], replicated, may hold values from 0.1 to 0.6
- w_qkv: bfloat16 [3072, 3, 1536], P(None, None, 'head')
- w_out: bfloat16 [1536, 3072], P('head'), may hold values from -0.15625 to 0.15625
Outputs:
- queue_out: bfloat16 [64, 512, 3072], P('queue', 'head')
The draws below stay inside these ranges and needn't reach their ends.
Inputs may be any that keep to these rules, and one draw needn't show every extreme that they name: `level_index`: the first position has level 0 and the last level 31.
All inputs are finite; a program needn't handle non-finite values.
Results may differ from the reference program's by a relative error of at most 0.0057.
Values may be sent and summed in bfloat16 or wider, within the bound.
No kernel may reach another device: no remote copies, remote signals or barrier semaphores. Data moves between devices by JAX's collectives and lax.ppermute only.
A program may use at most 128 MiB of HBM per device.

```python
import math
import jax
import jax.numpy as jnp
from jax import lax

D = 3072
HEADS = 12
HEAD_DIM = 128
TOK = 512
LEVELS = 32
ADV = 2
WIN = 256
FRAMES = 64


def draw_level_index(key, part):
    key = jax.random.fold_in(key, 11)
    spots = jnp.arange(FRAMES, dtype=jnp.int32)
    base = spots * LEVELS // FRAMES
    jitter = jax.random.randint(key, (FRAMES,), 0, 2, dtype=jnp.int32)
    levels = jnp.clip(base + jitter, 0, LEVELS - 1)
    levels = jnp.where(spots == 0, 0, levels)
    levels = jnp.where(spots == FRAMES - 1, LEVELS - 1, levels)
    return levels.astype(jnp.int32)


def draw_w_qkv(key, part):
    key = jax.random.fold_in(key, 23)
    first_key = jax.random.fold_in(key, 0)
    wide = HEADS * HEAD_DIM
    base = jax.random.normal(first_key, (D, 3, wide), jnp.float32) * D ** (-0.5)
    return base.astype(jnp.bfloat16)


def place_ends(array, rng, smallest, largest):
    longest = array.shape.index(max(array.shape))
    spots = []
    for shift in (0, 1):
        where = [jax.random.randint(jax.random.fold_in(rng, axis), (), 0, length) for axis, length in enumerate(array.shape)]
        where[longest] = (where[longest] + shift) % array.shape[longest]
        spots.append(tuple(where))
    return array.at[spots[0]].set(smallest).at[spots[1]].set(largest)


def steps_of(own_key, shape, pieces, smallest, high):
    level, own = 1.0, jax.random.fold_in(own_key, 6)
    for dim, shards_of in pieces:
        steps = jnp.exp(jax.random.uniform(jax.random.fold_in(own, dim), (shards_of,), jnp.float32, smallest / len(pieces), high / len(pieces)))
        level = level * jnp.repeat(steps, shape[dim] // shards_of).reshape([-1 if axis == dim else 1 for axis in range(len(shape))])
    return level


def scatter_about(key, dims, scale, most, cuts=(), held_as=jnp.bfloat16):
    loudness = steps_of(key, dims, cuts, -0.22, 0.18) if cuts else 1.0
    drawn = jax.random.normal(key, dims, jnp.float32) * scale * loudness
    return jnp.minimum(jnp.maximum(drawn, -most), most).astype(held_as)


def setup_inputs(seed: int = 0) -> dict:
    keys = jax.random.split(jax.random.key(seed), 9)
    latents = scatter_about(keys[0], (FRAMES, TOK, D), 1.0, 6.0, ((0, 64), (1, 4)))
    new_frame = scatter_about(keys[1], (TOK, D), 1.0, 6.0, ((0, 4),))
    level_index = draw_level_index(jax.random.fold_in(keys[8], 71), 0)
    window_offsets = place_ends(jax.random.randint(keys[3], (FRAMES, 2), 0, 3), jax.random.fold_in(keys[3], 1), 0, 2).astype(jnp.int32)
    mod_table = scatter_about(keys[4], (LEVELS, 3, D), 0.5, 3.0, (), jnp.float32)
    step_sizes = jnp.clip(jnp.exp(jax.random.uniform(keys[5], (LEVELS,), jnp.float32, math.log(0.1), math.log(0.6))), 0.1, 0.6)
    w_qkv = draw_w_qkv(jax.random.fold_in(keys[8], 71), 0)
    w_out = scatter_about(keys[7], (HEADS * HEAD_DIM, D), (HEADS * HEAD_DIM) ** -0.5, 0.15625, ((0, 4),))
    return {"latents": latents, "new_frame": new_frame, "level_index": level_index, "window_offsets": window_offsets, "mod_table": mod_table, "step_sizes": step_sizes, "w_qkv": w_qkv, "w_out": w_out}


epsilon = 1e-06

def normalize(state, chosen):
    values = state.astype(jnp.float32)
    average = lax.optimization_barrier(jnp.mean(values, axis=-1, keepdims=True))
    centered = values - average
    spread = lax.optimization_barrier(jnp.mean(centered * centered, axis=-1, keepdims=True))
    return (centered * lax.rsqrt(spread + epsilon) * (1.0 + chosen[1]) + chosen[0]).astype(jnp.bfloat16)

def reference(latents, new_frame, level_index, window_offsets, mod_table, step_sizes, w_qkv, w_out):
    wide = HEADS * HEAD_DIM
    quarter = TOK // 4
    frames = latents.shape[0]
    flat_w = w_qkv.reshape(D, 3 * wide)
    scaling = HEAD_DIM ** (-0.5)

    def project_frame(item):
        state, level_now = item
        normed = normalize(state, mod_table[level_now])
        return jnp.dot(normed, flat_w, preferred_element_type=jnp.float32).astype(jnp.bfloat16)

    def one_pass(queue_state):
        projected = lax.map(project_frame, (queue_state, level_index))
        queries_all = projected[:, :, :wide]
        keys_all = projected[:, :, wide:2 * wide]
        values_all = projected[:, :, 2 * wide:]

        def attend(frame):
            earlier = jnp.maximum(frame - 1, 0)
            later_idx = jnp.minimum(frame + 1, frames - 1)
            start_lo = (window_offsets[frame, 0] * quarter).astype(jnp.int32)
            start_hi = (window_offsets[frame, 1] * quarter).astype(jnp.int32)

            def context(table):
                own = lax.dynamic_index_in_dim(table, frame, 0, keepdims=False)
                before = lax.dynamic_index_in_dim(table, earlier, 0, keepdims=False)
                after = lax.dynamic_index_in_dim(table, later_idx, 0, keepdims=False)
                before = lax.dynamic_slice_in_dim(before, start_lo, WIN, 0)
                after = lax.dynamic_slice_in_dim(after, start_hi, WIN, 0)
                return jnp.concatenate([own, before, after], axis=0).reshape(-1, HEADS, HEAD_DIM)
            key_rows = context(keys_all)
            value_rows = context(values_all)
            queries = lax.dynamic_index_in_dim(queries_all, frame, 0, keepdims=False).reshape(TOK, HEADS, HEAD_DIM)
            allowed = jnp.concatenate([jnp.ones((TOK,), bool), jnp.full((WIN,), frame > 0), jnp.full((WIN,), frame < frames - 1)])
            scores = jnp.einsum('qhd,khd->hqk', queries.astype(jnp.float32), key_rows.astype(jnp.float32)) * scaling
            scores = jnp.where(allowed[None, None, :], scores, -jnp.inf)
            row_max = lax.optimization_barrier(jnp.max(scores, axis=-1, keepdims=True))
            weights = jnp.exp(scores - row_max)
            weights_bf = (weights / lax.optimization_barrier(jnp.sum(weights, axis=-1, keepdims=True))).astype(jnp.bfloat16)
            attended = jnp.einsum('hqk,khd->qhd', weights_bf.astype(jnp.float32), value_rows.astype(jnp.float32)).astype(jnp.bfloat16)
            attn = jnp.dot(attended.reshape(TOK, wide), w_out, preferred_element_type=jnp.float32)
            level_now = level_index[frame]
            chosen = mod_table[level_now]
            step_size = step_sizes[level_now]
            current = lax.dynamic_index_in_dim(queue_state, frame, 0, keepdims=False).astype(jnp.float32)
            return (current + step_size * (chosen[2] * attn - current)).astype(jnp.bfloat16)
        return lax.map(attend, jnp.arange(frames, dtype=jnp.int32))
    queue_state = latents
    for advance in range(ADV):
        if advance > 0:
            queue_state = jnp.concatenate([queue_state[1:], new_frame[None]], axis=0)
        queue_state = one_pass(queue_state)
    return queue_state
```

```python
import functools

import jax
import jax.numpy as jnp
from jax import lax
from jax.experimental import pallas as pl
from jax.experimental.pallas import tpu as pltpu
from jax.sharding import PartitionSpec as P

HEAD_DIM = 128
EPSILON = 1e-06
MIB = 1 << 20

SIDE = 4
PLACES = [(y, z, x) for y in range(SIDE) for z in range(SIDE) for x in range(SIDE)]
FRAMES = len(PLACES)


def place(y, z, x):
    return (y % SIDE * SIDE + z % SIDE) * SIDE + x % SIDE


CORE = [(i, i ^ 1) for i in range(4)]
CHIP = [(i, i ^ 2) for i in range(4)]
BOTH = [(i, i ^ 3) for i in range(4)]
UP = [(i, (i + 1) % FRAMES) for i in range(FRAMES)]
DOWN = [(target, source) for source, target in UP]
ROW_UP = [(place(y, z, x), place(y, z, x + 1)) for y, z, x in PLACES]
ROW_DOWN = [(place(y, z, x), place(y, z, x - 1)) for y, z, x in PLACES]


def row_of(frame, x):
    return frame % FRAMES // SIDE * SIDE + x


RELAY_UP = [(q, row_of(q + 1, SIDE - 1)) for q in range(FRAMES) if q % SIDE == SIDE - 1]
RELAY_DOWN = [(q, row_of(q - 1, 0)) for q in range(FRAMES) if q % SIDE == 0]
ACROSS = []
for y, z, x in PLACES:
    for core in range(2):
        ends = (place(y, z, x) * 4 + 2 + core, place(y, z + 1, x) * 4 + core)
        ACROSS += [ends, ends[::-1]]
COLUMNS = [[place(y, z, x) for y in range(SIDE)] for z in range(SIDE) for x in range(SIDE)]
EVERY = ("queue", "head")


def towards(step, mask):
    return [
        (q * 4 + h, (q + step) % FRAMES * 4 + (h ^ mask)) for q in range(FRAMES) for h in range(4)
    ]


def params(mib, *semantics):
    return pltpu.CompilerParams(
        vmem_limit_bytes=mib * MIB, dimension_semantics=semantics or ("arbitrary",)
    )


def normalized(values, modulation):
    average = jnp.mean(values, axis=-1, keepdims=True)
    centered = values - average
    spread = jnp.mean(centered * centered, axis=-1, keepdims=True)
    return (
        centered * lax.rsqrt(spread + EPSILON) * (1.0 + modulation[1:2]) + modulation[0:1]
    ).astype(jnp.bfloat16)


def norm_kernel(level, x_ref, mod_ref, out_ref):
    out_ref[...] = normalized(x_ref[...].astype(jnp.float32), mod_ref[0])


def norm(level, x, mod_table):
    rows, width = x.shape
    tile = 32
    return pl.pallas_call(
        norm_kernel,
        out_shape=jax.ShapeDtypeStruct((rows, width), jnp.bfloat16),
        grid_spec=pltpu.PrefetchScalarGridSpec(
            num_scalar_prefetch=1,
            grid=(rows // tile,),
            in_specs=[
                pl.BlockSpec((tile, width), lambda i, level: (i, 0)),
                pl.BlockSpec((1, 3, width), lambda i, level: (level[0], 0, 0)),
            ],
            out_specs=pl.BlockSpec((tile, width), lambda i, level: (i, 0)),
        ),
        compiler_params=params(24),
        cost_estimate=pl.CostEstimate(
            flops=10 * rows * width, bytes_accessed=4 * rows * width, transcendentals=rows
        ),
        name="norm",
    )(level, x, mod_table)


def project_kernel(a_ref, b_ref, w_ref, *rest):
    *out_refs, held = rest
    half = a_ref.shape[0]

    @pl.when(pl.program_id(0) == 0)
    def _():
        held[:half] = a_ref[...]
        held[half:] = b_ref[...]

    found = jnp.dot(held[...], w_ref[...], preferred_element_type=jnp.float32)
    for index, out_ref in enumerate(out_refs):

        @pl.when(pl.program_id(0) == index)
        def _():
            out_ref[...] = found.astype(jnp.bfloat16)


def project(a, b, weights, count):
    half, width = a.shape
    part = weights.shape[1] // count
    whole = pl.BlockSpec((half, width), lambda i: (0, 0))
    out = pl.BlockSpec((2 * half, part), lambda i: (0, 0))
    return pl.pallas_call(
        project_kernel,
        out_shape=[jax.ShapeDtypeStruct((2 * half, part), jnp.bfloat16)] * count,
        grid=(count,),
        in_specs=[whole, whole, pl.BlockSpec((width, part), lambda i: (0, i))],
        out_specs=[out] * count,
        scratch_shapes=[pltpu.VMEM((2 * half, width), jnp.bfloat16)],
        compiler_params=params(32),
        cost_estimate=pl.CostEstimate(
            flops=4 * half * width * part * count,
            bytes_accessed=2 * width * part * count + 4 * half * width,
            transcendentals=0,
        ),
        name="project",
    )(a, b, weights)


def attend_kernel(scaling, seen, q0, q1, k0, k1, v0, v1, kp, kn, vp, vn, out0, out1):
    keys = jnp.concatenate([k0[...], k1[...], kp[...], kn[...]], axis=0)
    values = jnp.concatenate([v0[...], v1[...], vp[...], vn[...]], axis=0)
    own = k0.shape[0] + k1.shape[0]
    window = kp.shape[0]
    spot = lax.broadcasted_iota(jnp.int32, (1, own + 2 * window), 1)
    hidden = ((spot >= own) & (spot < own + window) & (seen[0] == 0)) | (
        (spot >= own + window) & (seen[1] == 0)
    )
    shift = jnp.where(hidden, -jnp.inf, 0.0).astype(jnp.float32)
    for q_ref, out_ref in ((q0, out0), (q1, out1)):
        scores = lax.dot_general(
            q_ref[...], keys, (((1,), (1,)), ((), ())), preferred_element_type=jnp.float32
        )
        scores = scores * scaling + shift
        weights = jnp.exp2(scores - jnp.max(scores, axis=-1, keepdims=True))
        total = jnp.sum(weights, axis=-1, keepdims=True)
        found = jnp.dot(weights.astype(jnp.bfloat16), values, preferred_element_type=jnp.float32)
        out_ref[...] = (found / total).astype(jnp.bfloat16)


def attend(seen, q0, q1, k0, k1, v0, v1, kp, kn, vp, vn):
    rows, width = q0.shape
    window = kp.shape[0]
    full = pl.BlockSpec((rows, HEAD_DIM), lambda i, seen: (0, i))
    halo = pl.BlockSpec((window, HEAD_DIM), lambda i, seen: (0, i))
    keys = 2 * rows + 2 * window
    scaling = HEAD_DIM ** (-0.5) * 1.4426950408889634
    return pl.pallas_call(
        functools.partial(attend_kernel, scaling),
        out_shape=[jax.ShapeDtypeStruct((rows, width), jnp.bfloat16)] * 2,
        grid_spec=pltpu.PrefetchScalarGridSpec(
            num_scalar_prefetch=1,
            grid=(width // HEAD_DIM,),
            in_specs=[full] * 6 + [halo] * 4,
            out_specs=[full] * 2,
        ),
        compiler_params=params(40),
        cost_estimate=pl.CostEstimate(
            flops=8 * rows * keys * width,
            bytes_accessed=2 * 8 * rows * width,
            transcendentals=2 * rows * keys * (width // HEAD_DIM),
        ),
        name="attend",
    )(seen, q0, q1, k0, k1, v0, v1, kp, kn, vp, vn)


def advance_kernel(
    numbers, steps, a_self, a_core, a_chip, a_both, w_self, w_core, w_chip, w_both,
    x_own, x_chip, new_own, new_chip, gate_ref, mod_ref, state_ref, own_ref, chip_ref, held,
):
    half = x_own.shape[0]
    tile = x_own.shape[1]
    index = pl.program_id(0)
    step = steps[numbers[0]]
    gate = gate_ref[0, 2:3]

    def dot(a, b):
        return jnp.dot(a, b[...], preferred_element_type=jnp.float32)

    straight = dot(a_self[...], w_self) + dot(a_core[...], w_core)
    crossed = dot(a_chip[...], w_chip) + dot(a_both[...], w_both)
    columns = pl.ds(pl.multiple_of(index * tile, tile), tile)
    for place_in, x_ref, new_ref in ((0, x_own, new_own), (1, x_chip, new_chip)):
        here = slice(place_in * half, (place_in + 1) * half)
        there = slice((1 - place_in) * half, (2 - place_in) * half)
        attn = straight[here] + crossed[there]
        current = x_ref[...].astype(jnp.float32)
        state = (current + step * (gate * attn - current)).astype(jnp.bfloat16)
        state = jnp.where(numbers[2] == 1, new_ref[...], state)
        held[here, columns] = state
        if place_in == 0:
            state_ref[...] = state

    @pl.when(index == pl.num_programs(0) - 1)
    def _():
        chunk = 32
        for at in range(0, half, chunk):
            own_ref[at : at + chunk] = normalized(
                held[at : at + chunk].astype(jnp.float32), mod_ref[0]
            )
            chip_ref[at : at + chunk] = normalized(
                held[half + at : half + at + chunk].astype(jnp.float32), mod_ref[0]
            )


def advance(numbers, steps, attended, weights, x_own, x_chip, new_own, new_chip, mod_table):
    half, width = x_own.shape
    depth = weights[0].shape[0]
    tile = 512
    whole = pl.BlockSpec((2 * half, depth), lambda i, n, s: (0, 0))
    weight = pl.BlockSpec((depth, tile), lambda i, n, s: (0, i))
    piece = pl.BlockSpec((half, tile), lambda i, n, s: (0, i))
    out = pl.BlockSpec((half, width), lambda i, n, s: (0, 0))
    block = jax.ShapeDtypeStruct((half, width), jnp.bfloat16)
    return pl.pallas_call(
        advance_kernel,
        out_shape=[block] * 3,
        grid_spec=pltpu.PrefetchScalarGridSpec(
            num_scalar_prefetch=2,
            grid=(width // tile,),
            in_specs=[whole] * 4
            + [weight] * 4
            + [piece] * 4
            + [
                pl.BlockSpec((1, 3, tile), lambda i, n, s: (n[0], 0, i)),
                pl.BlockSpec((1, 3, width), lambda i, n, s: (n[1], 0, 0)),
            ],
            out_specs=[piece, out, out],
            scratch_shapes=[pltpu.VMEM((2 * half, width), jnp.bfloat16)],
        ),
        compiler_params=params(40),
        cost_estimate=pl.CostEstimate(
            flops=16 * half * depth * width,
            bytes_accessed=8 * depth * width + 14 * half * width,
            transcendentals=0,
        ),
        name="advance",
    )(numbers, steps, *attended, *weights, x_own, x_chip, new_own, new_chip, mod_table, mod_table)


def finish_kernel(
    numbers, steps, a_self, a_core, a_chip, a_both, w_self, w_core, w_chip, w_both,
    x_ref, gate_ref, out_ref,
):
    step = steps[numbers[0]]
    attn = 0.0
    for a, w in ((a_self, w_self), (a_core, w_core), (a_chip, w_chip), (a_both, w_both)):
        attn += jnp.dot(a[...], w[...], preferred_element_type=jnp.float32)
    current = x_ref[...].astype(jnp.float32)
    out_ref[0] = (current + step * (gate_ref[0, 2:3] * attn - current)).astype(jnp.bfloat16)


def finish(numbers, steps, attended, weights, x, mod_table):
    rows, width = x.shape
    depth = weights[0].shape[0]
    tile = 512
    whole = pl.BlockSpec((rows, depth), lambda i, n, s: (0, 0))
    weight = pl.BlockSpec((depth, tile), lambda i, n, s: (0, i))
    piece = pl.BlockSpec((rows, tile), lambda i, n, s: (0, i))
    return pl.pallas_call(
        finish_kernel,
        out_shape=jax.ShapeDtypeStruct((1, rows, width), jnp.bfloat16),
        grid_spec=pltpu.PrefetchScalarGridSpec(
            num_scalar_prefetch=2,
            grid=(width // tile,),
            in_specs=[whole] * 4
            + [weight] * 4
            + [piece, pl.BlockSpec((1, 3, tile), lambda i, n, s: (n[0], 0, i))],
            out_specs=pl.BlockSpec((1, rows, tile), lambda i, n, s: (0, 0, i)),
        ),
        compiler_params=params(32),
        cost_estimate=pl.CostEstimate(
            flops=8 * rows * depth * width,
            bytes_accessed=8 * depth * width + 4 * rows * width,
            transcendentals=0,
        ),
        name="finish",
    )(numbers, steps, *attended, *weights, x, mod_table)


def local(latents, new_frame, level_index, window_offsets, mod_table, step_sizes, w_qkv, w_out):
    frame = lax.axis_index("queue")
    head = lax.axis_index("head")
    along_x = lax.rem(frame, SIDE)
    along_y = frame // (SIDE * SIDE)
    x_own = latents[0]
    rows, width = x_own.shape
    part = w_qkv.shape[2]

    def head_permute(block, route):
        return lax.ppermute(block, "head", route)

    def queue_permute(block, route):
        return lax.ppermute(block, "queue", route)

    here = jnp.concatenate([level_index, window_offsets[0]])
    before = queue_permute(here, UP)
    after = queue_permute(here, DOWN)
    second = queue_permute(before, UP)

    x_chip = head_permute(x_own, CHIP)
    first_level = here[0:1]
    own = norm(first_level, x_own, mod_table)
    own_c = head_permute(own, CORE)

    quarter = w_out.shape[0] // SIDE
    share = lax.dynamic_slice_in_dim(w_out, along_y * quarter, quarter, 0)
    share = lax.ppermute(share, EVERY, ACROSS)
    w_chip = lax.all_gather(share, "queue", axis_index_groups=COLUMNS, axis=0, tiled=True)
    w_core = head_permute(w_out, CORE)
    w_both = head_permute(w_chip, CORE)
    w_all = (w_out, w_core, w_chip, w_both)

    new_chip = lax.ppermute(new_frame, EVERY, [(i, i ^ 2) for i in range(4)])

    w_q = w_qkv[:, 0]
    w_kv = w_qkv[:, 1:].reshape(width, 2 * part)

    def exchange(k, v, low, high):
        def window(blocks, start):
            def pick(index):
                slot = index ^ head
                slot = (slot >> 1) | ((slot & 1) << 1)
                return lax.dynamic_slice_in_dim(blocks, slot * rows, rows, 0)

            return jnp.concatenate([pick(start), pick(start + 1)], axis=0)

        k_up, k_down = window(k, low), window(k, high)
        v_up, v_down = window(v, low), window(v, high)
        relayed = queue_permute(jnp.where(along_x == 0, k_down, k_up), RELAY_UP + RELAY_DOWN)
        v_prev = queue_permute(v_up, UP)
        v_next = queue_permute(v_down, DOWN)
        k_prev = queue_permute(jnp.where(along_x == SIDE - 1, relayed, k_up), ROW_UP)
        k_next = queue_permute(jnp.where(along_x == 0, relayed, k_down), ROW_DOWN)
        return k_prev, k_next, v_prev, v_next

    def layer(own, chip, own_c, chip_c, early, low, high, seen):
        first, last = ((own, chip), (own_c, chip_c)) if not early else ((own, own_c), (chip, chip_c))
        k0, v0 = project(*first, w_kv, 2)
        (q0,) = project(*first, w_q, 1)
        k1, v1 = project(*last, w_kv, 2)
        (q1,) = project(*last, w_q, 1)
        if early:
            def order(a, b):
                return (
                    jnp.concatenate([a[:rows], b[:rows]], axis=0),
                    jnp.concatenate([a[rows:], b[rows:]], axis=0),
                )

            (q0, q1), (k0, k1), (v0, v1) = order(q0, q1), order(k0, k1), order(v0, v1)
        halo = exchange(
            jnp.concatenate([k0, k1], axis=0), jnp.concatenate([v0, v1], axis=0), low, high
        )
        return attend(seen, q0, q1, k0, k1, v0, v1, *halo)

    chip = norm(first_level, x_chip, mod_table)
    chip_c = head_permute(chip, CORE)
    seen = jnp.stack([frame > 0, frame < FRAMES - 1]).astype(jnp.int32)
    to_same, to_other = layer(own, chip, own_c, chip_c, True, after[1], before[2], seen)
    attended = (
        to_same,
        head_permute(to_other, CORE),
        head_permute(to_same, CHIP),
        head_permute(to_other, BOTH),
    )
    numbers = jnp.stack([here[0], before[0], (frame == 0).astype(jnp.int32)])
    state, own, chip = advance(
        numbers, step_sizes, attended, w_all, x_own, x_chip, new_frame, new_chip, mod_table
    )
    own_c = head_permute(own, CORE)
    chip_c = head_permute(chip, CORE)

    half = rows // 2
    relayed = queue_permute(state[half:], RELAY_DOWN)
    x_direct = queue_permute(state[:half], DOWN)
    x_rest = queue_permute(jnp.where(along_x == 0, relayed, state[half:]), ROW_DOWN)
    x_last = jnp.concatenate([x_direct, x_rest], axis=0)
    seen = jnp.stack([frame != 1, frame != 0]).astype(jnp.int32)
    to_same, to_other = layer(own, chip, own_c, chip_c, False, here[1], second[2], seen)
    attended = (
        lax.ppermute(to_same[:rows], EVERY, towards(-1, 0)),
        lax.ppermute(to_other[:rows], EVERY, towards(-1, 1)),
        lax.ppermute(to_same[rows:], EVERY, towards(-1, 2)),
        lax.ppermute(to_other[rows:], EVERY, towards(-1, 3)),
    )
    return finish(numbers, step_sizes, attended, w_all, x_last, mod_table)


def solution(mesh):
    return jax.shard_map(
        local,
        mesh=mesh,
        in_specs=(
            P("queue", "head", None),
            P("head", None),
            P("queue"),
            P("queue", None),
            P(),
            P(),
            P(None, None, "head"),
            P("head", None),
        ),
        out_specs=P("queue", "head", None),
        check_vma=False,
    )
```

```python
import functools

import jax
import jax.numpy as jnp
from jax import lax
from jax.experimental import pallas as pl
from jax.experimental.pallas import tpu as pltpu
from jax.sharding import PartitionSpec as P

HEAD_DIM = 128
EPSILON = 1e-06
MIB = 1 << 20

SIDE = 4
PLACES = [(y, z, x) for y in range(SIDE) for z in range(SIDE) for x in range(SIDE)]
FRAMES = len(PLACES)


def place(y, z, x):
    return (y % SIDE * SIDE + z % SIDE) * SIDE + x % SIDE


CORE = [(i, i ^ 1) for i in range(4)]
CHIP = [(i, i ^ 2) for i in range(4)]
BOTH = [(i, i ^ 3) for i in range(4)]
UP = [(i, (i + 1) % FRAMES) for i in range(FRAMES)]
DOWN = [(target, source) for source, target in UP]
ROW_UP = [(place(y, z, x), place(y, z, x + 1)) for y, z, x in PLACES]
ROW_DOWN = [(place(y, z, x), place(y, z, x - 1)) for y, z, x in PLACES]


def row_of(frame, x):
    return frame % FRAMES // SIDE * SIDE + x


RELAY_UP = [(q, row_of(q + 1, SIDE - 1)) for q in range(FRAMES) if q % SIDE == SIDE - 1]
RELAY_DOWN = [(q, row_of(q - 1, 0)) for q in range(FRAMES) if q % SIDE == 0]
ACROSS = []
for y, z, x in PLACES:
    for core in range(2):
        ends = (place(y, z, x) * 4 + 2 + core, place(y, z + 1, x) * 4 + core)
        ACROSS += [ends, ends[::-1]]
ALONG_Y_UP = [(place(y, z, x), place(y + 1, z, x)) for y, z, x in PLACES]
ALONG_Y_DOWN = [(place(y, z, x), place(y - 1, z, x)) for y, z, x in PLACES]
NEW_FRAME = [
    (place(0, z, 0) * 4 + side * 2 + core, (1 - side) * 2 + core)
    for z, side in ((SIDE - 1, 1), (1, 0))
    for core in range(2)
]
EVERY = ("queue", "head")


def towards(step, mask):
    return [
        (q * 4 + h, (q + step) % FRAMES * 4 + (h ^ mask)) for q in range(FRAMES) for h in range(4)
    ]


def limit(mib):
    return pltpu.CompilerParams(vmem_limit_bytes=mib * MIB)


VMEM = pl.BlockSpec(memory_space=pltpu.VMEM)
SMEM = pl.BlockSpec(memory_space=pltpu.SMEM)


def normalized(values, modulation):
    average = jnp.mean(values, axis=-1, keepdims=True)
    centered = values - average
    spread = jnp.mean(centered * centered, axis=-1, keepdims=True)
    return (
        centered * lax.rsqrt(spread + EPSILON) * (1.0 + modulation[1:2]) + modulation[0:1]
    ).astype(jnp.bfloat16)


def normalize_rows(x_ref, start, modulation, out_ref):
    chunk = 16

    def body(index, carry):
        at = pl.multiple_of(index * chunk, chunk)
        values = x_ref[pl.ds(start + at, chunk), :].astype(jnp.float32)
        out_ref[pl.ds(at, chunk), :] = normalized(values, modulation)
        return carry

    lax.fori_loop(0, out_ref.shape[0] // chunk, body, 0, unroll=4)


def norm_kernel(x_ref, mod_ref, out_ref):
    normalize_rows(x_ref, 0, mod_ref[0], out_ref)


def norm(x, modulation):
    rows, width = x.shape
    return pl.pallas_call(
        norm_kernel,
        out_shape=jax.ShapeDtypeStruct((rows, width), jnp.bfloat16),
        in_specs=[VMEM, VMEM],
        out_specs=VMEM,
        compiler_params=limit(8),
        cost_estimate=pl.CostEstimate(
            flops=10 * rows * width, bytes_accessed=4 * rows * width, transcendentals=rows
        ),
        name="norm",
    )(x, modulation)


def project_kernel(a_ref, b_ref, w_ref, *rest):
    *out_refs, held = rest
    half = a_ref.shape[0]
    part = out_refs[0].shape[1]
    held[:half] = a_ref[...]
    held[half:] = b_ref[...]
    for index, out_ref in enumerate(out_refs):
        out_ref[...] = jnp.dot(
            held[...],
            w_ref[:, index * part : (index + 1) * part],
            preferred_element_type=jnp.float32,
        ).astype(jnp.bfloat16)


def project(a, b, weights, count):
    half, width = a.shape
    part = weights.shape[1] // count
    return pl.pallas_call(
        project_kernel,
        out_shape=[jax.ShapeDtypeStruct((2 * half, part), jnp.bfloat16)] * count,
        in_specs=[VMEM] * 3,
        out_specs=[VMEM] * count,
        scratch_shapes=[pltpu.VMEM((2 * half, width), jnp.bfloat16)],
        compiler_params=limit(14),
        cost_estimate=pl.CostEstimate(
            flops=4 * half * width * part * count,
            bytes_accessed=2 * width * part * count + 4 * half * width,
            transcendentals=0,
        ),
        name="project",
    )(a, b, weights)


def attend_kernel(scaling, seen, q0, q1, k0, k1, v0, v1, kp, kn, vp, vn, out0, out1):
    keys = jnp.concatenate([k0[...], k1[...], kp[...], kn[...]], axis=0)
    values = jnp.concatenate([v0[...], v1[...], vp[...], vn[...]], axis=0)
    own = k0.shape[0] + k1.shape[0]
    window = kp.shape[0]
    spot = lax.broadcasted_iota(jnp.int32, (1, own + 2 * window), 1)
    hidden = ((spot >= own) & (spot < own + window) & (seen[0] == 0)) | (
        (spot >= own + window) & (seen[1] == 0)
    )
    shift = jnp.where(hidden, -jnp.inf, 0.0).astype(jnp.float32)
    for q_ref, out_ref in ((q0, out0), (q1, out1)):
        scores = lax.dot_general(
            q_ref[...], keys, (((1,), (1,)), ((), ())), preferred_element_type=jnp.float32
        )
        scores = scores * scaling + shift
        weights = jnp.exp2(scores - jnp.max(scores, axis=-1, keepdims=True))
        total = jnp.sum(weights, axis=-1, keepdims=True)
        found = jnp.dot(weights.astype(jnp.bfloat16), values, preferred_element_type=jnp.float32)
        out_ref[...] = (found / total).astype(jnp.bfloat16)


def attend(seen, q0, q1, k0, k1, v0, v1, kp, kn, vp, vn):
    rows, width = q0.shape
    window = kp.shape[0]
    full = pl.BlockSpec((rows, HEAD_DIM), lambda i, seen: (0, i))
    halo = pl.BlockSpec((window, HEAD_DIM), lambda i, seen: (0, i))
    keys = 2 * rows + 2 * window
    scaling = HEAD_DIM ** (-0.5) * 1.4426950408889634
    return pl.pallas_call(
        functools.partial(attend_kernel, scaling),
        out_shape=[jax.ShapeDtypeStruct((rows, width), jnp.bfloat16)] * 2,
        grid_spec=pltpu.PrefetchScalarGridSpec(
            num_scalar_prefetch=1,
            grid=(width // HEAD_DIM,),
            in_specs=[full] * 6 + [halo] * 4,
            out_specs=[full] * 2,
        ),
        compiler_params=limit(16),
        cost_estimate=pl.CostEstimate(
            flops=8 * rows * keys * width,
            bytes_accessed=2 * 8 * rows * width,
            transcendentals=2 * rows * keys * (width // HEAD_DIM),
        ),
        name="attend",
    )(seen, q0, q1, k0, k1, v0, v1, kp, kn, vp, vn)


def tiles(along_y, pieces):
    own, low, high, first, second = pieces
    tile = first[0].shape[1]
    found = []
    for offset, refs in ((0, own), (SIDE - 1, low), (1, high)):
        start = lax.rem(along_y + offset, SIDE) * (2 * tile)
        found += [(start + at, refs, at) for at in (0, tile)]
    start = lax.rem(along_y + 2, SIDE) * (2 * tile)
    return tile, found + [(start, first, 0), (start + tile, second, 0)]


def dot(a, b):
    return jnp.dot(a, b, preferred_element_type=jnp.float32)


def advance_kernel(numbers, steps, *refs):
    a_self, a_core, a_chip, a_both, w_self, w_core = refs[:6]
    pieces = list(zip(refs[6:11], refs[11:16]))
    x_own, x_chip, new_own, new_chip, gate_ref, mod_ref, state_ref, own_ref, chip_ref, held = refs[16:]
    half = x_own.shape[0]
    step = steps[numbers[0]]
    fresh = numbers[1] == 1
    tile, found = tiles(numbers[2], pieces)
    for start, (chip, both), at in found:
        columns = pl.ds(pl.multiple_of(start, tile), tile)
        straight = dot(a_self[...], w_self[:, columns]) + dot(a_core[...], w_core[:, columns])
        crossed = dot(a_chip[...], chip[:, at : at + tile]) + dot(
            a_both[...], both[:, at : at + tile]
        )
        gate = gate_ref[0, 2:3, columns]
        for low, x_ref, new_ref in ((0, x_own, new_own), (half, x_chip, new_chip)):
            attn = straight[low : low + half] + crossed[half - low : 2 * half - low]
            current = x_ref[:, columns].astype(jnp.float32)
            state = (current + step * (gate * attn - current)).astype(jnp.bfloat16)
            held[low : low + half, columns] = jnp.where(fresh, new_ref[:, columns], state)
    state_ref[...] = held[:half]
    normalize_rows(held, 0, mod_ref[0], own_ref)
    normalize_rows(held, half, mod_ref[0], chip_ref)


def advance(numbers, steps, attended, weights, x_own, x_chip, new_own, new_chip, gate, modulation):
    half, width = x_own.shape
    depth = attended[0].shape[1]
    block = jax.ShapeDtypeStruct((half, width), jnp.bfloat16)
    return pl.pallas_call(
        advance_kernel,
        out_shape=[block] * 3,
        in_specs=[SMEM] * 2 + [VMEM] * 22,
        out_specs=[VMEM] * 3,
        scratch_shapes=[pltpu.VMEM((2 * half, width), jnp.bfloat16)],
        compiler_params=limit(24),
        cost_estimate=pl.CostEstimate(
            flops=16 * half * depth * width,
            bytes_accessed=8 * depth * width + 14 * half * width,
            transcendentals=0,
        ),
        name="advance",
    )(numbers, steps, *attended, *weights, x_own, x_chip, new_own, new_chip, gate, modulation)


def finish_kernel(numbers, steps, *refs):
    a_self, a_core, a_chip, a_both, w_self, w_core = refs[:6]
    pieces = list(zip(refs[6:11], refs[11:16]))
    x_ref, gate_ref, out_ref = refs[16:]
    step = steps[numbers[0]]
    tile, found = tiles(numbers[2], pieces)
    for start, (chip, both), at in found:
        columns = pl.ds(pl.multiple_of(start, tile), tile)
        attn = dot(a_self[...], w_self[:, columns]) + dot(a_core[...], w_core[:, columns])
        attn += dot(a_chip[...], chip[:, at : at + tile])
        attn += dot(a_both[...], both[:, at : at + tile])
        current = x_ref[:, columns].astype(jnp.float32)
        gate = gate_ref[0, 2:3, columns]
        out_ref[0, :, columns] = (current + step * (gate * attn - current)).astype(jnp.bfloat16)


def finish(numbers, steps, attended, weights, x, gate):
    rows, width = x.shape
    depth = attended[0].shape[1]
    return pl.pallas_call(
        finish_kernel,
        out_shape=jax.ShapeDtypeStruct((1, rows, width), jnp.bfloat16),
        in_specs=[SMEM] * 2 + [VMEM] * 18,
        out_specs=VMEM,
        compiler_params=limit(20),
        cost_estimate=pl.CostEstimate(
            flops=8 * rows * depth * width,
            bytes_accessed=8 * depth * width + 4 * rows * width,
            transcendentals=0,
        ),
        name="finish",
    )(numbers, steps, *attended, *weights, x, gate)


def local(latents, new_frame, level_index, window_offsets, mod_table, step_sizes, w_qkv, w_out):
    frame = lax.axis_index("queue")
    head = lax.axis_index("head")
    along_x = lax.rem(frame, SIDE)
    along_y = frame // (SIDE * SIDE)
    x_own = latents[0]
    rows, width = x_own.shape
    part = w_qkv.shape[2]

    def head_permute(block, route):
        return lax.ppermute(block, "head", route)

    def queue_permute(block, route):
        return lax.ppermute(block, "queue", route)

    def modulation(level):
        return lax.dynamic_slice_in_dim(mod_table, level, 1, 0)

    here = jnp.concatenate([level_index, window_offsets[0]])
    before = queue_permute(here, UP)
    after = queue_permute(here, DOWN)
    second = queue_permute(before, UP)

    x_chip = head_permute(x_own, CHIP)
    quarter = width // SIDE
    share = lax.dynamic_slice_in_dim(w_out, along_y * quarter, quarter, 1)
    share = lax.ppermute(share, EVERY, ACROSS)

    mod_now = modulation(here[0])
    own = norm(x_own, mod_now)
    own_c = head_permute(own, CORE)
    w_kv = w_qkv[:, 1:].reshape(width, 2 * part)
    w_q = w_qkv[:, 0]
    k0, v0 = project(own, own_c, w_kv, 2)
    (q0,) = project(own, own_c, w_q, 1)
    x_chip, share, second, after, before, k0, v0, q0 = lax.optimization_barrier(
        (x_chip, share, second, after, before, k0, v0, q0)
    )
    mod_next = modulation(before[0])

    chip = norm(x_chip, mod_now)
    chip_c = head_permute(chip, CORE)

    share_low = queue_permute(share, ALONG_Y_UP)
    share_high = queue_permute(share, ALONG_Y_DOWN)
    new_chip = lax.ppermute(new_frame, EVERY, NEW_FRAME)
    w_core = head_permute(w_out, CORE)

    def exchange(k, v, low, high, *beside):
        def window(blocks, start):
            def pick(index):
                slot = index ^ head
                slot = (slot >> 1) | ((slot & 1) << 1)
                return lax.dynamic_slice_in_dim(blocks, slot * rows, rows, 0)

            return jnp.concatenate([pick(start), pick(start + 1)], axis=0)

        k_up, k_down = window(k, low), window(k, high)
        v_up, v_down = window(v, low), window(v, high)
        relayed = queue_permute(jnp.where(along_x == 0, k_down, k_up), RELAY_UP + RELAY_DOWN)
        v_prev = queue_permute(v_up, UP)
        v_next = queue_permute(v_down, DOWN)
        relayed, v_prev, v_next, beside = lax.optimization_barrier(
            (relayed, v_prev, v_next, beside)
        )
        k_prev = queue_permute(jnp.where(along_x == SIDE - 1, relayed, k_up), ROW_UP)
        k_next = queue_permute(jnp.where(along_x == 0, relayed, k_down), ROW_DOWN)
        return (k_prev, k_next, v_prev, v_next), beside

    def order(a, b):
        return (
            jnp.concatenate([a[:rows], b[:rows]], axis=0),
            jnp.concatenate([a[rows:], b[rows:]], axis=0),
        )

    k1, v1 = project(chip, chip_c, w_kv, 2)
    (q1,) = project(chip, chip_c, w_q, 1)
    (q0, q1), (k0, k1), (v0, v1) = order(q0, q1), order(k0, k1), order(v0, v1)
    halo, (share_low, share_high) = exchange(
        jnp.concatenate([k0, k1], axis=0),
        jnp.concatenate([v0, v1], axis=0),
        after[1],
        before[2],
        share_low,
        share_high,
    )
    share_first = queue_permute(share_low[:, : quarter // 2], ALONG_Y_UP)
    share_second = queue_permute(share_high[:, quarter // 2 :], ALONG_Y_DOWN)
    halo, share_first, share_second = lax.optimization_barrier((halo, share_first, share_second))
    w_chip = (share, share_low, share_high, share_first, share_second)
    w_both = tuple(head_permute(piece, CORE) for piece in w_chip)
    w_all = (w_out, w_core, *w_chip, *w_both)
    seen = jnp.stack([frame > 0, frame < FRAMES - 1]).astype(jnp.int32)
    to_same, to_other = attend(seen, q0, q1, k0, k1, v0, v1, *halo)
    attended = (
        to_same,
        head_permute(to_other, CORE),
        head_permute(to_same, CHIP),
        head_permute(to_other, BOTH),
    )
    numbers = jnp.stack([here[0], (frame == 0).astype(jnp.int32), along_y])
    state, own, chip = advance(
        numbers, step_sizes, attended, w_all, x_own, x_chip, new_frame, new_chip, mod_now, mod_next
    )

    own_c = head_permute(own, CORE)
    chip_c = head_permute(chip, CORE)
    half = rows // 2
    relayed = queue_permute(state[half:], RELAY_DOWN)
    x_direct = queue_permute(state[:half], DOWN)
    k0, v0 = project(own, chip, w_kv, 2)
    (q0,) = project(own, chip, w_q, 1)
    k1, v1 = project(own_c, chip_c, w_kv, 2)
    (q1,) = project(own_c, chip_c, w_q, 1)
    halo, (relayed,) = exchange(
        jnp.concatenate([k0, k1], axis=0),
        jnp.concatenate([v0, v1], axis=0),
        here[1],
        second[2],
        relayed,
    )
    x_rest = queue_permute(jnp.where(along_x == 0, relayed, state[half:]), ROW_DOWN)
    halo, x_direct, x_rest = lax.optimization_barrier((halo, x_direct, x_rest))
    x_last = jnp.concatenate([x_direct, x_rest], axis=0)
    seen = jnp.stack([frame != 1, frame != 0]).astype(jnp.int32)
    to_same, to_other = attend(seen, q0, q1, k0, k1, v0, v1, *halo)
    attended = (
        lax.ppermute(to_same[:rows], EVERY, towards(-1, 0)),
        lax.ppermute(to_other[:rows], EVERY, towards(-1, 1)),
        lax.ppermute(to_same[rows:], EVERY, towards(-1, 2)),
        lax.ppermute(to_other[rows:], EVERY, towards(-1, 3)),
    )
    return finish(numbers, step_sizes, attended, w_all, x_last, mod_now)


def solution(mesh):
    return jax.shard_map(
        local,
        mesh=mesh,
        in_specs=(
            P("queue", "head", None),
            P("head", None),
            P("queue"),
            P("queue", None),
            P(),
            P(),
            P(None, None, "head"),
            P("head", None),
        ),
        out_specs=P("queue", "head", None),
        check_vma=False,
    )
```

```python
import functools

import jax
import jax.numpy as jnp
from jax import lax
from jax.experimental import pallas as pl
from jax.experimental.pallas import tpu as pltpu
from jax.sharding import PartitionSpec as P

HEAD_DIM = 128
EPSILON = 1e-06
MIB = 1 << 20

SIDE = 4
PLACES = [(y, z, x) for y in range(SIDE) for z in range(SIDE) for x in range(SIDE)]
FRAMES = len(PLACES)


def place(y, z, x):
    return (y % SIDE * SIDE + z % SIDE) * SIDE + x % SIDE


CORE = [(i, i ^ 1) for i in range(4)]
CHIP = [(i, i ^ 2) for i in range(4)]
BOTH = [(i, i ^ 3) for i in range(4)]
UP = [(i, (i + 1) % FRAMES) for i in range(FRAMES)]
DOWN = [(target, source) for source, target in UP]
UP_TWICE = [(i, (i + 2) % FRAMES) for i in range(FRAMES)]


def row_of(frame, x):
    return frame % FRAMES // SIDE * SIDE + x


ROW_UP = [(place(y, z, x), place(y, z, x + 1)) for y, z, x in PLACES]
ROW_DOWN = [(target, source) for source, target in ROW_UP]
FIRST_UP = [(q, row_of(q + SIDE, 0)) for q in range(FRAMES) if q % SIDE == 0]
LAST_DOWN = [(q, row_of(q - SIDE, SIDE - 1)) for q in range(FRAMES) if q % SIDE == SIDE - 1]
ACROSS = []
for y, z, x in PLACES:
    for core in range(2):
        ends = (place(y, z, x) * 4 + 2 + core, place(y, z + 1, x) * 4 + core)
        ACROSS += [ends, ends[::-1]]
ALONG_Y_UP = [(place(y, z, x), place(y + 1, z, x)) for y, z, x in PLACES]
ALONG_Y_DOWN = [(place(y, z, x), place(y - 1, z, x)) for y, z, x in PLACES]
NEW_FRAME = [
    (place(0, z, 0) * 4 + side * 2 + core, (1 - side) * 2 + core)
    for z, side in ((SIDE - 1, 1), (1, 0))
    for core in range(2)
]
EVERY = ("queue", "head")


def towards(step, mask):
    return [
        (q * 4 + h, (q + step) % FRAMES * 4 + (h ^ mask)) for q in range(FRAMES) for h in range(4)
    ]


def limit(mib):
    return pltpu.CompilerParams(vmem_limit_bytes=mib * MIB)


VMEM = pl.BlockSpec(memory_space=pltpu.VMEM)
SMEM = pl.BlockSpec(memory_space=pltpu.SMEM)
ANY = pl.BlockSpec(memory_space=pl.ANY)


def normalized(values, modulation):
    average = jnp.mean(values, axis=-1, keepdims=True)
    centered = values - average
    spread = jnp.mean(centered * centered, axis=-1, keepdims=True)
    return (
        centered * lax.rsqrt(spread + EPSILON) * (1.0 + modulation[1:2]) + modulation[0:1]
    ).astype(jnp.bfloat16)


def normalize_rows(x_ref, modulation, out_ref):
    chunk = 16

    def body(index, carry):
        at = pl.multiple_of(index * chunk, chunk)
        values = x_ref[pl.ds(at, chunk), :].astype(jnp.float32)
        out_ref[pl.ds(at, chunk), :] = normalized(values, modulation)
        return carry

    lax.fori_loop(0, x_ref.shape[0] // chunk, body, 0, unroll=4)


def dot(a, b):
    return jnp.dot(a, b, preferred_element_type=jnp.float32)


def norm_kernel(x_ref, mod_ref, out_ref):
    normalize_rows(x_ref, mod_ref[0], out_ref)


def norm(x, modulation):
    rows, width = x.shape
    return pl.pallas_call(
        norm_kernel,
        out_shape=jax.ShapeDtypeStruct((rows, width), jnp.bfloat16),
        in_specs=[VMEM] * 2,
        out_specs=VMEM,
        compiler_params=limit(8),
        cost_estimate=pl.CostEstimate(
            flops=10 * rows * width, bytes_accessed=4 * rows * width, transcendentals=rows
        ),
        name="norm",
    )(x, modulation)


def resident_kernel(*refs):
    *pairs, sems = refs
    count = len(pairs) // 2
    copies = [
        pltpu.make_async_copy(source, target, sems.at[i])
        for i, (source, target) in enumerate(zip(pairs[:count], pairs[count:]))
    ]
    for copy in copies:
        copy.start()
    for copy in copies:
        copy.wait()


def resident(*arrays):
    return pl.pallas_call(
        resident_kernel,
        out_shape=[pltpu.VMEM(x.shape, x.dtype) for x in arrays],
        in_specs=[ANY] * len(arrays),
        out_specs=[VMEM] * len(arrays),
        scratch_shapes=[pltpu.SemaphoreType.DMA((len(arrays),))],
        compiler_params=limit(4),
        cost_estimate=pl.CostEstimate(
            flops=0, bytes_accessed=4 * sum(x.size for x in arrays), transcendentals=0
        ),
        name="resident",
    )(*arrays)


def queries_kernel(*refs):
    *x_refs, w_ref, out_ref = refs
    for i, x_ref in enumerate(x_refs):
        rows = x_ref.shape[0]
        out_ref[i * rows : (i + 1) * rows] = dot(x_ref[...], w_ref[...]).astype(jnp.bfloat16)


def keys_kernel(slots, *refs):
    x_refs, w_ref = refs[:4], refs[4]
    k_ref, v_ref, k_up, k_down, v_up, v_down = refs[5:]
    rows = x_refs[0].shape[0]
    part = k_ref.shape[1]
    for i, x_ref in enumerate(x_refs):
        here = slice(i * rows, (i + 1) * rows)
        found = dot(x_ref[...], w_ref[...]).astype(jnp.bfloat16)
        k_ref[here] = found[:, :part]
        v_ref[here] = found[:, part:]
    for i in range(2):
        here = slice(i * rows, (i + 1) * rows)
        up = pl.ds(pl.multiple_of(slots[i] * rows, rows), rows)
        down = pl.ds(pl.multiple_of(slots[2 + i] * rows, rows), rows)
        k_up[here] = k_ref[up, :]
        v_up[here] = v_ref[up, :]
        k_down[here] = k_ref[down, :]
        v_down[here] = v_ref[down, :]


def queries(blocks, weights):
    rows, width = blocks[0].shape
    part = weights.shape[1]
    return pl.pallas_call(
        queries_kernel,
        out_shape=jax.ShapeDtypeStruct((4 * rows, part), jnp.bfloat16),
        in_specs=[VMEM] * 5,
        out_specs=VMEM,
        compiler_params=limit(14),
        cost_estimate=pl.CostEstimate(
            flops=8 * rows * width * part,
            bytes_accessed=2 * width * part + 8 * rows * width,
            transcendentals=0,
        ),
        name="queries",
    )(*blocks, weights)


def keys(slots, blocks, weights):
    rows, width = blocks[0].shape
    part = weights.shape[1] // 2
    whole = jax.ShapeDtypeStruct((4 * rows, part), jnp.bfloat16)
    window = jax.ShapeDtypeStruct((2 * rows, part), jnp.bfloat16)
    return pl.pallas_call(
        keys_kernel,
        out_shape=[whole] * 2 + [window] * 4,
        in_specs=[SMEM] + [VMEM] * 5,
        out_specs=[VMEM] * 6,
        compiler_params=limit(18),
        cost_estimate=pl.CostEstimate(
            flops=16 * rows * width * part,
            bytes_accessed=4 * width * part + 8 * rows * width,
            transcendentals=0,
        ),
        name="keys",
    )(slots, *blocks, weights)


def attend_kernel(scaling, seen, q, k, v, kp, kn, ends, vp, vn, out0, out1):
    k_prev = jnp.where(seen[2] == 1, ends[...], kp[...])
    k_next = jnp.where(seen[3] == 1, ends[...], kn[...])
    keys = jnp.concatenate([k[...], k_prev, k_next], axis=0)
    values = jnp.concatenate([v[...], vp[...], vn[...]], axis=0)
    values = jnp.concatenate([values, jnp.ones_like(values)], axis=1)
    own, window = k.shape[0], kp.shape[0]
    spot = lax.broadcasted_iota(jnp.int32, (1, 2 * window), 1)
    hidden = ((spot < window) & (seen[0] == 0)) | ((spot >= window) & (seen[1] == 0))
    shift = jnp.where(hidden, -jnp.inf, 0.0).astype(jnp.float32)
    rows = out0.shape[0]
    for part in range(2):
        scores = lax.dot_general(
            q[part * rows : (part + 1) * rows],
            keys,
            (((1,), (1,)), ((), ())),
            preferred_element_type=jnp.float32,
        )
        inside, beside = scores[:, :own], scores[:, own:] + shift
        highest = jnp.maximum(
            jnp.max(inside, axis=-1, keepdims=True), jnp.max(beside, axis=-1, keepdims=True)
        )
        weights = jnp.concatenate(
            [
                jnp.exp2((inside - highest) * scaling).astype(jnp.bfloat16),
                jnp.exp2((beside - highest) * scaling).astype(jnp.bfloat16),
            ],
            axis=1,
        )
        found = dot(weights, values)
        found = found[:, :HEAD_DIM] / found[:, HEAD_DIM:]
        (out0, out1)[part][...] = found.astype(jnp.bfloat16)


def attend(seen, q, k, v, kp, kn, ends, vp, vn):
    rows, width = q.shape
    window = kp.shape[0]
    full = pl.BlockSpec((rows, HEAD_DIM), lambda i, seen: (0, i))
    halo = pl.BlockSpec((window, HEAD_DIM), lambda i, seen: (0, i))
    out = pl.BlockSpec((rows // 2, HEAD_DIM), lambda i, seen: (0, i))
    depth = rows + 2 * window
    scaling = HEAD_DIM ** (-0.5) * 1.4426950408889634
    return pl.pallas_call(
        functools.partial(attend_kernel, scaling),
        out_shape=[jax.ShapeDtypeStruct((rows // 2, width), jnp.bfloat16)] * 2,
        grid_spec=pltpu.PrefetchScalarGridSpec(
            num_scalar_prefetch=1,
            grid=(width // HEAD_DIM,),
            in_specs=[full] * 3 + [halo] * 5,
            out_specs=[out] * 2,
        ),
        compiler_params=limit(16),
        cost_estimate=pl.CostEstimate(
            flops=4 * rows * depth * width,
            bytes_accessed=2 * 8 * rows * width,
            transcendentals=rows * depth * (width // HEAD_DIM),
        ),
        name="attend",
    )(seen, q, k, v, kp, kn, ends, vp, vn)


def run_copies(pairs, sems):
    copies = [
        pltpu.make_async_copy(source, target, sems.at[i])
        for i, (source, target) in enumerate(pairs)
    ]
    for copy in copies:
        copy.start()
    for copy in copies:
        copy.wait()


def assemble_kernel(own, low, high, first, second, out, sems):
    half = first.shape[1]
    pairs = [(own, out.at[0]), (low, out.at[1]), (high, out.at[2])]
    pairs += [(first, out.at[3, :, :half]), (second, out.at[3, :, half:])]
    run_copies(pairs, sems)


def assemble(*pieces):
    depth, tile = pieces[0].shape
    return pl.pallas_call(
        assemble_kernel,
        out_shape=jax.ShapeDtypeStruct((SIDE, depth, tile), jnp.bfloat16),
        in_specs=[ANY] * 5,
        out_specs=ANY,
        scratch_shapes=[pltpu.SemaphoreType.DMA((5,))],
        compiler_params=limit(4),
        cost_estimate=pl.CostEstimate(
            flops=0, bytes_accessed=4 * SIDE * depth * tile, transcendentals=0
        ),
        name="assemble",
    )(*pieces)


def gather_kernel(along_y, w_self, w_core, w_chip, w_both, buffer, sems):
    depth = w_self.shape[0]
    tile = buffer.shape[2]
    pairs = []
    for index, columns in enumerate(tile_columns(along_y[0], tile)):
        for i, source in enumerate(
            (w_self.at[:, columns], w_core.at[:, columns], w_chip.at[index], w_both.at[index])
        ):
            pairs.append((source, buffer.at[index, i * depth : (i + 1) * depth]))
    run_copies(pairs, sems)


def gather_weights(along_y, w_self, *weights):
    depth, width = w_self.shape
    return pl.pallas_call(
        gather_kernel,
        out_shape=pltpu.VMEM((SIDE, 4 * depth, width // SIDE), jnp.bfloat16),
        in_specs=[SMEM] + [ANY] * 4,
        out_specs=VMEM,
        scratch_shapes=[pltpu.SemaphoreType.DMA((4 * SIDE,))],
        compiler_params=limit(4),
        cost_estimate=pl.CostEstimate(
            flops=0, bytes_accessed=16 * depth * width, transcendentals=0
        ),
        name="gather_weights",
    )(along_y, w_self, *weights)


def tile_columns(along_y, tile):
    return [
        pl.ds(pl.multiple_of(lax.rem(along_y + offset, SIDE) * tile, tile), tile)
        for offset in (0, SIDE - 1, 1, 2)
    ]


def advance_kernel(numbers, steps, *refs):
    attended, weights = refs[:4], refs[4]
    x_refs, (new_own, new_chip, gate_ref, mod_ref) = refs[5:7], refs[7:11]
    state_ref, own_ref, chip_ref, heads, held = refs[11:]
    half = own_ref.shape[0]
    depth = attended[0].shape[1]
    for i, ref in enumerate(attended):
        columns = slice(i * depth, (i + 1) * depth)
        if i < 2:
            heads[:, columns] = ref[...]
        else:
            heads[:half, columns] = ref[half:]
            heads[half:, columns] = ref[:half]
    step = steps[numbers[0]]
    fresh = numbers[1] == 1
    for index, columns in enumerate(tile_columns(numbers[2], weights.shape[2])):
        attn = dot(heads[...], weights[index])
        current = jnp.concatenate([x_ref[:, columns] for x_ref in x_refs], axis=0)
        current = current.astype(jnp.float32)
        gate = gate_ref[0, 2:3, columns]
        state = (current + step * (gate * attn - current)).astype(jnp.bfloat16)
        new = jnp.concatenate([new_own[:, columns], new_chip[:, columns]], axis=0)
        held[:, columns] = jnp.where(fresh, new, state)
    state_ref[...] = held[:half]
    normalize_rows(held.at[:half], mod_ref[0], own_ref)
    normalize_rows(held.at[half:], mod_ref[0], chip_ref)


def advance(numbers, steps, attended, weights, x_parts, new_own, new_chip, gate, modulation):
    half, width = new_own.shape
    depth = attended[0].shape[1]
    block = jax.ShapeDtypeStruct((half, width), jnp.bfloat16)
    return pl.pallas_call(
        advance_kernel,
        out_shape=[block] * 3,
        in_specs=[SMEM] * 2 + [VMEM] * 11,
        out_specs=[VMEM] * 3,
        scratch_shapes=[
            pltpu.VMEM((2 * half, 4 * depth), jnp.bfloat16),
            pltpu.VMEM((2 * half, width), jnp.bfloat16),
        ],
        compiler_params=limit(20),
        cost_estimate=pl.CostEstimate(
            flops=16 * half * depth * width,
            bytes_accessed=14 * half * width,
            transcendentals=0,
        ),
        name="advance",
    )(numbers, steps, *attended, weights, *x_parts, new_own, new_chip, gate, modulation)


def finish_kernel(numbers, steps, *refs):
    attended, (weights, x_ref, gate_ref, out_ref, heads) = refs[:4], refs[4:]
    depth = attended[0].shape[1]
    for i, ref in enumerate(attended):
        heads[:, i * depth : (i + 1) * depth] = ref[...]
    step = steps[numbers[0]]
    for index, columns in enumerate(tile_columns(numbers[2], weights.shape[2])):
        attn = dot(heads[...], weights[index])
        current = x_ref[:, columns].astype(jnp.float32)
        gate = gate_ref[0, 2:3, columns]
        out_ref[0, :, columns] = (current + step * (gate * attn - current)).astype(jnp.bfloat16)


def finish(numbers, steps, attended, weights, x, gate):
    rows, width = x.shape
    depth = attended[0].shape[1]
    return pl.pallas_call(
        finish_kernel,
        out_shape=jax.ShapeDtypeStruct((1, rows, width), jnp.bfloat16),
        in_specs=[SMEM] * 2 + [VMEM] * 7,
        out_specs=VMEM,
        scratch_shapes=[pltpu.VMEM((rows, 4 * depth), jnp.bfloat16)],
        compiler_params=limit(14),
        cost_estimate=pl.CostEstimate(
            flops=8 * rows * depth * width, bytes_accessed=4 * rows * width, transcendentals=0
        ),
        name="finish",
    )(numbers, steps, *attended, weights, x, gate)


def local(latents, new_frame, level_index, window_offsets, mod_table, step_sizes, w_qkv, w_out):
    frame = lax.axis_index("queue")
    head = lax.axis_index("head")
    along_x = lax.rem(frame, SIDE)
    along_y = frame // (SIDE * SIDE)
    rows, width = latents.shape[1:]
    part = w_qkv.shape[2]
    first_in_row = (along_x == 0).astype(jnp.int32)
    last_in_row = (along_x == SIDE - 1).astype(jnp.int32)

    def head_permute(block, route):
        return lax.ppermute(block, "head", route)

    def queue_permute(block, route):
        return lax.ppermute(block, "queue", route)

    def modulation(level):
        return lax.dynamic_slice_in_dim(mod_table, level, 1, 0)

    x_own = latents[0]
    x_chip = head_permute(x_own, CHIP)
    quarter = width // SIDE
    share = lax.dynamic_slice_in_dim(w_out, along_y * quarter, quarter, 1)
    share = lax.ppermute(share, EVERY, ACROSS)
    here = jnp.concatenate([level_index, window_offsets[0]])
    after = queue_permute(here, DOWN)
    before = queue_permute(here, UP)
    second = queue_permute(here, UP_TWICE)
    w_kv = w_qkv[:, 1:].reshape(width, 2 * part)
    w_q = w_qkv[:, 0]
    w_kv, w_q = resident(w_kv, w_q)
    mod_first = modulation(here[0])
    own = norm(x_own, mod_first)
    own_c = head_permute(own, CORE)
    x_chip, share, after, before, second, own_c, w_kv, w_q, w_late, new_frame = (
        lax.optimization_barrier(
            (x_chip, share, after, before, second, own_c, w_kv, w_q, w_out, new_frame)
        )
    )
    share_low = queue_permute(share, ALONG_Y_UP)
    share_high = queue_permute(share, ALONG_Y_DOWN)
    chip = norm(x_chip, mod_first)
    chip_c = head_permute(chip, CORE)
    mod_last = modulation(before[0])

    def layer(blocks, low, high, seen, *beside):
        def slot(index):
            index = index ^ head
            return (index >> 1) | ((index & 1) << 1)

        slots = jnp.stack([slot(low), slot(low + 1), slot(high), slot(high + 1)])
        k, v, k_up, k_down, v_up, v_down = keys(slots, blocks, w_kv)
        v_prev = queue_permute(v_up, UP)
        v_next = queue_permute(v_down, DOWN)
        k_prev = queue_permute(k_up, ROW_UP)
        k_next = queue_permute(k_down, ROW_DOWN)
        k_prev, k_next, beside = lax.optimization_barrier((k_prev, k_next, beside))
        ends = jnp.where(along_x == 0, k_prev, k_next)
        ends = queue_permute(ends, FIRST_UP + LAST_DOWN)
        q = queries(blocks, w_q)
        seen = jnp.stack([*(x.astype(jnp.int32) for x in seen), first_in_row, last_in_row])
        return *attend(seen, q, k, v, k_prev, k_next, ends, v_prev, v_next), beside

    to_same, to_other, (share_low, share_high) = layer(
        (own, chip, own_c, chip_c),
        after[1],
        before[2],
        (frame > 0, frame < FRAMES - 1),
        share_low,
        share_high,
    )
    share_first = queue_permute(share_low[:, : quarter // 2], ALONG_Y_UP)
    share_second = queue_permute(share_high[:, quarter // 2 :], ALONG_Y_DOWN)
    w_core = head_permute(w_late, CORE)
    new_chip = lax.ppermute(new_frame, EVERY, NEW_FRAME)
    w_chip = assemble(share, share_low, share_high, share_first, share_second)
    to_same, to_other, w_chip, w_core, new_chip = lax.optimization_barrier(
        (to_same, to_other, w_chip, w_core, new_chip)
    )
    w_both = head_permute(w_chip, CORE)
    attended = (
        to_same,
        head_permute(to_other, CORE),
        head_permute(to_same, CHIP),
        head_permute(to_other, BOTH),
    )
    w_all = gather_weights(along_y[None], w_out, w_core, w_chip, w_both)
    numbers = jnp.stack([here[0], (frame == 0).astype(jnp.int32), along_y])
    state, own, chip = advance(
        numbers, step_sizes, attended, w_all, (x_own, x_chip), new_frame, new_chip, mod_first, mod_last
    )

    own_c = head_permute(own, CORE)
    chip_c = head_permute(chip, CORE)
    x_last = queue_permute(state, DOWN)
    to_same, to_other, _ = layer(
        (own, chip, own_c, chip_c), here[1], second[2], (frame != 1, frame != 0)
    )
    to_same, to_other, x_last = lax.optimization_barrier((to_same, to_other, x_last))
    attended = (
        lax.ppermute(to_same[:rows], EVERY, towards(-1, 0)),
        lax.ppermute(to_other[:rows], EVERY, towards(-1, 1)),
        lax.ppermute(to_same[rows:], EVERY, towards(-1, 2)),
        lax.ppermute(to_other[rows:], EVERY, towards(-1, 3)),
    )
    return finish(numbers, step_sizes, attended, w_all, x_last, mod_first)


def solution(mesh):
    return jax.shard_map(
        local,
        mesh=mesh,
        in_specs=(
            P("queue", "head", None),
            P("head", None),
            P("queue"),
            P("queue", None),
            P(),
            P(),
            P(None, None, "head"),
            P("head", None),
        ),
        out_specs=P("queue", "head", None),
        check_vma=False,
    )
```

```python
import functools

import jax
import jax.numpy as jnp
from jax import lax
from jax.experimental import pallas as pl
from jax.experimental.pallas import tpu as pltpu
from jax.sharding import PartitionSpec as P

HEAD_DIM = 128
EPSILON = 1e-06
MIB = 1 << 20

SIDE = 4
PLACES = [(y, z, x) for y in range(SIDE) for z in range(SIDE) for x in range(SIDE)]
FRAMES = len(PLACES)


def place(y, z, x):
    return (y % SIDE * SIDE + z % SIDE) * SIDE + x % SIDE


CORE = [(i, i ^ 1) for i in range(4)]
CHIP = [(i, i ^ 2) for i in range(4)]
BOTH = [(i, i ^ 3) for i in range(4)]
UP = [(i, (i + 1) % FRAMES) for i in range(FRAMES)]
DOWN = [(target, source) for source, target in UP]
UP_TWICE = [(i, (i + 2) % FRAMES) for i in range(FRAMES)]


def row_of(frame, x):
    return frame % FRAMES // SIDE * SIDE + x


ROW_UP = [(place(y, z, x), place(y, z, x + 1)) for y, z, x in PLACES]
ROW_DOWN = [(target, source) for source, target in ROW_UP]
FIRST_UP = [(q, row_of(q + SIDE, 0)) for q in range(FRAMES) if q % SIDE == 0]
LAST_DOWN = [(q, row_of(q - SIDE, SIDE - 1)) for q in range(FRAMES) if q % SIDE == SIDE - 1]
ACROSS = []
for y, z, x in PLACES:
    for core in range(2):
        ends = (place(y, z, x) * 4 + 2 + core, place(y, z + 1, x) * 4 + core)
        ACROSS += [ends, ends[::-1]]
ALONG_Y_UP = [(place(y, z, x), place(y + 1, z, x)) for y, z, x in PLACES]
ALONG_Y_DOWN = [(place(y, z, x), place(y - 1, z, x)) for y, z, x in PLACES]
NEW_FRAME = [
    (place(0, z, 0) * 4 + side * 2 + core, (1 - side) * 2 + core)
    for z, side in ((SIDE - 1, 1), (1, 0))
    for core in range(2)
]
EVERY = ("queue", "head")


def towards(step, mask):
    return [
        (q * 4 + h, (q + step) % FRAMES * 4 + (h ^ mask)) for q in range(FRAMES) for h in range(4)
    ]


def limit(mib):
    return pltpu.CompilerParams(vmem_limit_bytes=mib * MIB)


VMEM = pl.BlockSpec(memory_space=pltpu.VMEM)
SMEM = pl.BlockSpec(memory_space=pltpu.SMEM)
HBM = pl.BlockSpec(memory_space=pltpu.HBM)


def normalized(values, modulation):
    average = jnp.mean(values, axis=-1, keepdims=True)
    centered = values - average
    spread = jnp.mean(centered * centered, axis=-1, keepdims=True)
    return (
        centered * lax.rsqrt(spread + EPSILON) * (1.0 + modulation[1:2]) + modulation[0:1]
    ).astype(jnp.bfloat16)


def normalize_rows(x_ref, modulation, out_ref):
    chunk = 16

    def body(index, carry):
        at = pl.multiple_of(index * chunk, chunk)
        values = x_ref[pl.ds(at, chunk), :].astype(jnp.float32)
        out_ref[pl.ds(at, chunk), :] = normalized(values, modulation)
        return carry

    lax.fori_loop(0, x_ref.shape[0] // chunk, body, 0, unroll=4)


def dot(a, b):
    return jnp.dot(a, b, preferred_element_type=jnp.float32)


def norm_kernel(x_ref, mod_ref, out_ref):
    normalize_rows(x_ref, mod_ref[0], out_ref)


def norm(x, modulation):
    rows, width = x.shape
    return pl.pallas_call(
        norm_kernel,
        out_shape=jax.ShapeDtypeStruct((rows, width), jnp.bfloat16),
        in_specs=[VMEM] * 2,
        out_specs=VMEM,
        compiler_params=limit(8),
        cost_estimate=pl.CostEstimate(
            flops=10 * rows * width, bytes_accessed=4 * rows * width, transcendentals=rows
        ),
        name="norm",
    )(x, modulation)


def queries_kernel(*refs):
    *x_refs, w_ref, out_ref = refs
    for i, x_ref in enumerate(x_refs):
        rows = x_ref.shape[0]
        out_ref[i * rows : (i + 1) * rows] = dot(x_ref[...], w_ref[...]).astype(jnp.bfloat16)


def keys_kernel(slots, *refs):
    x_refs, (wk_ref, wv_ref), (k_ref, v_ref, k_up, k_down, v_up, v_down, mixed) = (
        refs[:4],
        refs[4:6],
        refs[6:],
    )
    rows = x_refs[0].shape[0]
    whole = mixed.shape[1]
    rest = whole // 2
    mixed[:, :rest] = wk_ref[:, whole:]
    mixed[:, rest:] = wv_ref[:, whole:]
    for i, x_ref in enumerate(x_refs):
        here = slice(i * rows, (i + 1) * rows)
        k_ref[here, :whole] = dot(x_ref[...], wk_ref[:, :whole]).astype(jnp.bfloat16)
        v_ref[here, :whole] = dot(x_ref[...], wv_ref[:, :whole]).astype(jnp.bfloat16)
        found = dot(x_ref[...], mixed[...]).astype(jnp.bfloat16)
        k_ref[here, whole:] = found[:, :rest]
        v_ref[here, whole:] = found[:, rest:]
    for i in range(2):
        here = slice(i * rows, (i + 1) * rows)
        up = pl.ds(pl.multiple_of(slots[i] * rows, rows), rows)
        down = pl.ds(pl.multiple_of(slots[2 + i] * rows, rows), rows)
        k_up[here] = k_ref[up, :]
        v_up[here] = v_ref[up, :]
        k_down[here] = k_ref[down, :]
        v_down[here] = v_ref[down, :]


def queries(blocks, weights):
    rows, width = blocks[0].shape
    part = weights.shape[1]
    return pl.pallas_call(
        queries_kernel,
        out_shape=jax.ShapeDtypeStruct((4 * rows, part), jnp.bfloat16),
        in_specs=[VMEM] * 5,
        out_specs=VMEM,
        compiler_params=limit(14),
        cost_estimate=pl.CostEstimate(
            flops=8 * rows * width * part,
            bytes_accessed=2 * width * part + 8 * rows * width,
            transcendentals=0,
        ),
        name="queries",
    )(*blocks, weights)


def keys(slots, blocks, weights):
    rows, width = blocks[0].shape
    part = weights[0].shape[1]
    whole = jax.ShapeDtypeStruct((4 * rows, part), jnp.bfloat16)
    window = jax.ShapeDtypeStruct((2 * rows, part), jnp.bfloat16)
    return pl.pallas_call(
        keys_kernel,
        out_shape=[whole] * 2 + [window] * 4,
        in_specs=[SMEM] + [VMEM] * 6,
        out_specs=[VMEM] * 6,
        scratch_shapes=[pltpu.VMEM((width, 2 * part // 3), jnp.bfloat16)],
        compiler_params=limit(18),
        cost_estimate=pl.CostEstimate(
            flops=16 * rows * width * part,
            bytes_accessed=4 * width * part + 8 * rows * width,
            transcendentals=0,
        ),
        name="keys",
    )(slots, *blocks, *weights)


SCALING = HEAD_DIM ** (-0.5) * 1.4426950408889634


def weighted(scores, highest, values):
    weights = jnp.exp2((scores - highest) * SCALING).astype(jnp.bfloat16)
    return dot(weights, jnp.concatenate([values, jnp.ones_like(values)], axis=1))


def score(queries, keys):
    return lax.dot_general(
        queries, keys, (((1,), (1,)), ((), ())), preferred_element_type=jnp.float32
    )


def attend_own_kernel(q, k, v, sums, totals, peaks):
    rows = q.shape[0] // 2
    for part in range(2):
        here = slice(part * rows, (part + 1) * rows)
        scores = score(q[here], k[...])
        highest = jnp.max(scores, axis=-1, keepdims=True)
        found = weighted(scores, highest, v[...])
        sums[here] = found[:, :HEAD_DIM]
        totals[here] = found[:, HEAD_DIM:]
        peaks[here] = jnp.broadcast_to(highest, (rows, HEAD_DIM))


def attend_own(q, k, v):
    rows, width = q.shape
    full = pl.BlockSpec((rows, HEAD_DIM), lambda i: (0, i))
    return pl.pallas_call(
        attend_own_kernel,
        out_shape=[jax.ShapeDtypeStruct((rows, width), jnp.float32)] * 3,
        grid=(width // HEAD_DIM,),
        in_specs=[full] * 3,
        out_specs=[full] * 3,
        compiler_params=limit(16),
        cost_estimate=pl.CostEstimate(
            flops=4 * rows * rows * width,
            bytes_accessed=18 * rows * width,
            transcendentals=rows * rows * (width // HEAD_DIM),
        ),
        name="attend_own",
    )(q, k, v)


def attend_kernel(seen, q, sums, totals, peaks, kp, kn, k_ends, vp, vn, out0, out1):
    k_prev = jnp.where(seen[2] == 1, k_ends[...], kp[...])
    k_next = jnp.where(seen[3] == 1, k_ends[...], kn[...])
    keys = jnp.concatenate([k_prev, k_next], axis=0)
    values = jnp.concatenate([vp[...], vn[...]], axis=0)
    window = kp.shape[0]
    spot = lax.broadcasted_iota(jnp.int32, (1, 2 * window), 1)
    hidden = ((spot < window) & (seen[0] == 0)) | ((spot >= window) & (seen[1] == 0))
    shift = jnp.where(hidden, -jnp.inf, 0.0).astype(jnp.float32)
    rows = out0.shape[0]
    for part in range(2):
        here = slice(part * rows, (part + 1) * rows)
        scores = score(q[here], keys) + shift
        peak = peaks[here]
        highest = jnp.maximum(peak[:, :1], jnp.max(scores, axis=-1, keepdims=True))
        found = weighted(scores, highest, values)
        before = jnp.exp2((peak - highest) * SCALING)
        total = totals[here] * before + found[:, HEAD_DIM:]
        found = sums[here] * before + found[:, :HEAD_DIM]
        (out0, out1)[part][...] = (found / total).astype(jnp.bfloat16)


def attend(seen, q, own, kp, kn, k_ends, vp, vn):
    rows, width = q.shape
    window = kp.shape[0]
    full = pl.BlockSpec((rows, HEAD_DIM), lambda i, seen: (0, i))
    halo = pl.BlockSpec((window, HEAD_DIM), lambda i, seen: (0, i))
    out = pl.BlockSpec((rows // 2, HEAD_DIM), lambda i, seen: (0, i))
    return pl.pallas_call(
        attend_kernel,
        out_shape=[jax.ShapeDtypeStruct((rows // 2, width), jnp.bfloat16)] * 2,
        grid_spec=pltpu.PrefetchScalarGridSpec(
            num_scalar_prefetch=1,
            grid=(width // HEAD_DIM,),
            in_specs=[full] * 4 + [halo] * 5,
            out_specs=[out] * 2,
        ),
        compiler_params=limit(16),
        cost_estimate=pl.CostEstimate(
            flops=8 * rows * window * width,
            bytes_accessed=20 * rows * width,
            transcendentals=2 * rows * window * (width // HEAD_DIM),
        ),
        name="attend",
    )(seen, q, *own, kp, kn, k_ends, vp, vn)


def run_copies(pairs, sems):
    copies = [
        pltpu.make_async_copy(source, target, sems.at[i])
        for i, (source, target) in enumerate(pairs)
    ]
    for copy in copies:
        copy.start()
    for copy in copies:
        copy.wait()


def gather_kernel(along_y, w_self, w_core, *refs):
    *pieces, buffer, sems = refs
    depth = w_self.shape[0]
    tile = buffer.shape[2]
    pairs = []
    for index, columns in enumerate(tile_columns(along_y[0], tile)):
        sources = (w_self.at[:, columns], w_core.at[:, columns], pieces[index], pieces[SIDE + index])
        for i, source in enumerate(sources):
            pairs.append((source, buffer.at[index, i * depth : (i + 1) * depth]))
    run_copies(pairs, sems)


def gather_weights(along_y, w_self, *weights):
    depth, width = w_self.shape
    return pl.pallas_call(
        gather_kernel,
        out_shape=pltpu.VMEM((SIDE, 4 * depth, width // SIDE), jnp.bfloat16),
        in_specs=[SMEM] + [HBM] * 10,
        out_specs=VMEM,
        scratch_shapes=[pltpu.SemaphoreType.DMA((4 * SIDE,))],
        compiler_params=limit(4),
        cost_estimate=pl.CostEstimate(
            flops=0, bytes_accessed=16 * depth * width, transcendentals=0
        ),
        name="gather_weights",
    )(along_y, w_self, *weights)


def tile_columns(along_y, tile):
    return [
        pl.ds(pl.multiple_of(lax.rem(along_y + offset, SIDE) * tile, tile), tile)
        for offset in (0, SIDE - 1, 1, 2)
    ]


def advance_kernel(numbers, steps, *refs):
    attended, weights = refs[:4], refs[4]
    x_refs, (new_own, new_chip, gate_ref, mod_ref) = refs[5:7], refs[7:11]
    state_ref, own_ref, chip_ref, heads, held = refs[11:]
    half = own_ref.shape[0]
    depth = attended[0].shape[1]
    for i, ref in enumerate(attended):
        columns = slice(i * depth, (i + 1) * depth)
        if i < 2:
            heads[:, columns] = ref[...]
        else:
            heads[:half, columns] = ref[half:]
            heads[half:, columns] = ref[:half]
    step = steps[numbers[0]]
    fresh = numbers[1] == 1
    for index, columns in enumerate(tile_columns(numbers[2], weights.shape[2])):
        attn = dot(heads[...], weights[index])
        current = jnp.concatenate([x_ref[:, columns] for x_ref in x_refs], axis=0)
        current = current.astype(jnp.float32)
        gate = gate_ref[0, 2:3, columns]
        state = (current + step * (gate * attn - current)).astype(jnp.bfloat16)
        new = jnp.concatenate([new_own[:, columns], new_chip[:, columns]], axis=0)
        held[:, columns] = jnp.where(fresh, new, state)
    state_ref[...] = held[:half]
    normalize_rows(held.at[:half], mod_ref[0], own_ref)
    normalize_rows(held.at[half:], mod_ref[0], chip_ref)


def advance(numbers, steps, attended, weights, x_parts, new_own, new_chip, gate, modulation):
    half, width = new_own.shape
    depth = attended[0].shape[1]
    block = jax.ShapeDtypeStruct((half, width), jnp.bfloat16)
    return pl.pallas_call(
        advance_kernel,
        out_shape=[block] * 3,
        in_specs=[SMEM] * 2 + [VMEM] * 11,
        out_specs=[VMEM] * 3,
        scratch_shapes=[
            pltpu.VMEM((2 * half, 4 * depth), jnp.bfloat16),
            pltpu.VMEM((2 * half, width), jnp.bfloat16),
        ],
        compiler_params=limit(20),
        cost_estimate=pl.CostEstimate(
            flops=16 * half * depth * width,
            bytes_accessed=14 * half * width,
            transcendentals=0,
        ),
        name="advance",
    )(numbers, steps, *attended, weights, *x_parts, new_own, new_chip, gate, modulation)


def finish_kernel(numbers, steps, *refs):
    attended, (weights, first, late, ends, gate_ref, out_ref, heads) = refs[:4], refs[4:]
    depth = attended[0].shape[1]
    for i, ref in enumerate(attended):
        heads[:, i * depth : (i + 1) * depth] = ref[...]
    step = steps[numbers[0]]
    for index, columns in enumerate(tile_columns(numbers[2], weights.shape[2])):
        attn = dot(heads[...], weights[index])
        rest = jnp.where(numbers[1] == 1, ends[:, columns], late[:, columns])
        current = jnp.concatenate([first[:, columns], rest], axis=0).astype(jnp.float32)
        gate = gate_ref[0, 2:3, columns]
        out_ref[0, :, columns] = (current + step * (gate * attn - current)).astype(jnp.bfloat16)


def finish(numbers, steps, attended, weights, x_parts, gate):
    rows, depth = attended[0].shape
    width = gate.shape[2]
    return pl.pallas_call(
        finish_kernel,
        out_shape=jax.ShapeDtypeStruct((1, rows, width), jnp.bfloat16),
        in_specs=[SMEM] * 2 + [VMEM] * 9,
        out_specs=VMEM,
        scratch_shapes=[pltpu.VMEM((rows, 4 * depth), jnp.bfloat16)],
        compiler_params=limit(14),
        cost_estimate=pl.CostEstimate(
            flops=8 * rows * depth * width, bytes_accessed=4 * rows * width, transcendentals=0
        ),
        name="finish",
    )(numbers, steps, *attended, weights, *x_parts, gate)


def local(latents, new_frame, level_index, window_offsets, mod_table, step_sizes, w_qkv, w_out):
    frame = lax.axis_index("queue")
    head = lax.axis_index("head")
    along_x = lax.rem(frame, SIDE)
    along_y = frame // (SIDE * SIDE)
    rows, width = latents.shape[1:]
    part = w_qkv.shape[2]

    def head_permute(block, route):
        return lax.ppermute(block, "head", route)

    def queue_permute(block, route):
        return lax.ppermute(block, "queue", route)

    def modulation(level):
        return lax.dynamic_slice_in_dim(mod_table, level, 1, 0)

    x_own = latents[0]
    x_chip = head_permute(x_own, CHIP)
    here = jnp.concatenate([level_index, window_offsets[0]])
    after = queue_permute(here, DOWN)
    before = queue_permute(here, UP)
    second = queue_permute(here, UP_TWICE)
    mod_first = modulation(level_index[0])
    own = norm(x_own, mod_first)
    own, after, before, w_out, w_qkv = lax.optimization_barrier(
        (own, after, before, w_out, w_qkv)
    )
    own_c = head_permute(own, CORE)
    quarter = width // SIDE
    share = lax.dynamic_slice_in_dim(w_out, along_y * quarter, quarter, 1)
    share = lax.ppermute(share, EVERY, ACROSS)
    w_q, w_k, w_v = (w_qkv[:, i] for i in range(3))
    w_core = head_permute(w_out, CORE)
    x_chip, share, own_c, w_q, w_k, w_v, w_core = lax.optimization_barrier(
        (x_chip, share, own_c, w_q, w_k, w_v, w_core)
    )
    chip = norm(x_chip, mod_first)
    chip_c = head_permute(chip, CORE)
    mod_last = modulation(before[0])

    def windows(blocks, low, high, weights):
        def slot(index):
            index = index ^ head
            return (index >> 1) | ((index & 1) << 1)

        slots = jnp.stack([slot(low), slot(low + 1), slot(high), slot(high + 1)])
        return keys(slots, blocks, weights)

    def between_rows(k_prev, k_next):
        ends = jnp.where(along_x == 0, k_prev, k_next)
        return queue_permute(ends, FIRST_UP + LAST_DOWN)

    def shown(prev, after):
        flags = (prev, after, along_x == 0, along_x == SIDE - 1)
        return jnp.stack([flag.astype(jnp.int32) for flag in flags])

    blocks = (own, chip, own_c, chip_c)
    share_low = queue_permute(share, ALONG_Y_UP)
    share_high = queue_permute(share, ALONG_Y_DOWN)
    new_chip = lax.ppermute(new_frame, EVERY, NEW_FRAME)
    k, v, k_up, k_down, v_up, v_down = windows(blocks, after[1], before[2], (w_k, w_v))
    v_prev = queue_permute(v_up, UP)
    v_next = queue_permute(v_down, DOWN)
    k_prev = queue_permute(k_up, ROW_UP)
    k_next = queue_permute(k_down, ROW_DOWN)
    k_ends = between_rows(k_prev, k_next)
    w_q_now, share_low, share_high, new_chip = lax.optimization_barrier(
        (w_q, share_low, share_high, new_chip)
    )
    q = queries(blocks, w_q_now)
    inside = attend_own(q, k, v)
    share_far = queue_permute(share_low, ALONG_Y_UP)
    seen = shown(frame > 0, frame < FRAMES - 1)
    to_same, to_other = attend(seen, q, inside, k_prev, k_next, k_ends, v_prev, v_next)
    to_same, to_other, share_far, second = lax.optimization_barrier(
        (to_same, to_other, share_far, second)
    )
    attended = (
        to_same,
        head_permute(to_other, CORE),
        head_permute(to_same, CHIP),
        head_permute(to_other, BOTH),
    )
    w_chip = (share, share_low, share_high, share_far)
    w_both = tuple(head_permute(piece, CORE) for piece in w_chip)
    w_rows = (w_out, w_core, *w_chip, *w_both)
    w_all = gather_weights(along_y[None], *w_rows)
    numbers = jnp.stack([here[0], (frame == 0).astype(jnp.int32), along_y])
    state, own, chip = advance(
        numbers, step_sizes, attended, w_all, (x_own, x_chip), new_frame, new_chip, mod_first, mod_last
    )

    own, chip, w_rows = lax.optimization_barrier((own, chip, w_rows))
    own_c = head_permute(own, CORE)
    chip_c = head_permute(chip, CORE)
    half = rows // 2
    x_late = queue_permute(state[half:], ROW_DOWN)
    x_first = queue_permute(state[:half], DOWN)
    blocks = (own, chip, own_c, chip_c)
    k, v, k_up, k_down, v_up, v_down = windows(blocks, here[1], second[2], (w_k, w_v))
    v_prev = queue_permute(v_up, UP)
    v_next = queue_permute(v_down, DOWN)
    k_prev = queue_permute(k_up, ROW_UP)
    k_next = queue_permute(k_down, ROW_DOWN)
    k_ends = between_rows(k_prev, k_next)
    q = queries(blocks, w_q)
    inside = attend_own(q, k, v)
    inside, x_first, x_late = lax.optimization_barrier((inside, x_first, x_late))
    seen = shown(frame != 1, frame != 0)
    to_same, to_other = attend(seen, q, inside, k_prev, k_next, k_ends, v_prev, v_next)
    to_same, to_other, w_rows, x_late = lax.optimization_barrier(
        (to_same, to_other, w_rows, x_late)
    )
    x_ends = queue_permute(x_late, LAST_DOWN)
    attended = (
        lax.ppermute(to_same[:rows], EVERY, towards(-1, 0)),
        lax.ppermute(to_other[:rows], EVERY, towards(-1, 1)),
        lax.ppermute(to_same[rows:], EVERY, towards(-1, 2)),
        lax.ppermute(to_other[rows:], EVERY, towards(-1, 3)),
    )
    w_all = gather_weights(along_y[None], *w_rows)
    numbers = jnp.stack([here[0], (along_x == SIDE - 1).astype(jnp.int32), along_y])
    x_parts = (x_first, x_late, x_ends)
    return finish(numbers, step_sizes, attended, w_all, x_parts, mod_first)


def solution(mesh):
    return jax.shard_map(
        local,
        mesh=mesh,
        in_specs=(
            P("queue", "head", None),
            P("head", None),
            P("queue"),
            P("queue", None),
            P(),
            P(),
            P(None, None, "head"),
            P("head", None),
        ),
        out_specs=P("queue", "head", None),
        check_vma=False,
    )
```

```python
import functools

import jax
import jax.numpy as jnp
from jax import lax
from jax.experimental import pallas as pl
from jax.experimental.pallas import tpu as pltpu
from jax.sharding import PartitionSpec as P

HEAD_DIM = 128
EPSILON = 1e-06
MIB = 1 << 20

SIDE = 4
PLACES = [(y, z, x) for y in range(SIDE) for z in range(SIDE) for x in range(SIDE)]
FRAMES = len(PLACES)


def place(y, z, x):
    return (y % SIDE * SIDE + z % SIDE) * SIDE + x % SIDE


CORE = [(i, i ^ 1) for i in range(4)]
CHIP = [(i, i ^ 2) for i in range(4)]
BOTH = [(i, i ^ 3) for i in range(4)]
UP = [(i, (i + 1) % FRAMES) for i in range(FRAMES)]
DOWN = [(target, source) for source, target in UP]
UP_TWICE = [(i, (i + 2) % FRAMES) for i in range(FRAMES)]


def row_of(frame, x):
    return frame % FRAMES // SIDE * SIDE + x


ROW_UP = [(place(y, z, x), place(y, z, x + 1)) for y, z, x in PLACES]
ROW_DOWN = [(target, source) for source, target in ROW_UP]
FIRST_UP = [(q, row_of(q + SIDE, 0)) for q in range(FRAMES) if q % SIDE == 0]
LAST_DOWN = [(q, row_of(q - SIDE, SIDE - 1)) for q in range(FRAMES) if q % SIDE == SIDE - 1]
ACROSS = []
for y, z, x in PLACES:
    for core in range(2):
        ends = (place(y, z, x) * 4 + 2 + core, place(y, z + 1, x) * 4 + core)
        ACROSS += [ends, ends[::-1]]
ALONG_Y_UP = [(place(y, z, x), place(y + 1, z, x)) for y, z, x in PLACES]
ALONG_Y_DOWN = [(place(y, z, x), place(y - 1, z, x)) for y, z, x in PLACES]
NEW_FRAME = [
    (place(0, z, 0) * 4 + side * 2 + core, (1 - side) * 2 + core)
    for z, side in ((SIDE - 1, 1), (1, 0))
    for core in range(2)
]
EVERY = ("queue", "head")


def towards(step, mask):
    return [
        (q * 4 + h, (q + step) % FRAMES * 4 + (h ^ mask)) for q in range(FRAMES) for h in range(4)
    ]


def limit(mib):
    return pltpu.CompilerParams(vmem_limit_bytes=mib * MIB)


VMEM = pl.BlockSpec(memory_space=pltpu.VMEM)
SMEM = pl.BlockSpec(memory_space=pltpu.SMEM)
HBM = pl.BlockSpec(memory_space=pltpu.HBM)


def normalized(values, modulation):
    average = jnp.mean(values, axis=-1, keepdims=True)
    centered = values - average
    spread = jnp.mean(centered * centered, axis=-1, keepdims=True)
    return (
        centered * lax.rsqrt(spread + EPSILON) * (1.0 + modulation[1:2]) + modulation[0:1]
    ).astype(jnp.bfloat16)


def normalize_rows(x_ref, modulation, out_ref):
    chunk = 16

    def body(index, carry):
        at = pl.multiple_of(index * chunk, chunk)
        values = x_ref[pl.ds(at, chunk), :].astype(jnp.float32)
        out_ref[pl.ds(at, chunk), :] = normalized(values, modulation)
        return carry

    lax.fori_loop(0, x_ref.shape[0] // chunk, body, 0, unroll=4)


def dot(a, b):
    return jnp.dot(a, b, preferred_element_type=jnp.float32)


def norm_kernel(x_ref, mod_ref, out_ref):
    normalize_rows(x_ref, mod_ref[0], out_ref)


def norm(x, modulation):
    rows, width = x.shape
    return pl.pallas_call(
        norm_kernel,
        out_shape=jax.ShapeDtypeStruct((rows, width), jnp.bfloat16),
        in_specs=[VMEM] * 2,
        out_specs=VMEM,
        compiler_params=limit(8),
        cost_estimate=pl.CostEstimate(
            flops=10 * rows * width, bytes_accessed=4 * rows * width, transcendentals=rows
        ),
        name="norm",
    )(x, modulation)


def queries_kernel(*refs):
    *x_refs, w_ref, out_ref = refs
    for i, x_ref in enumerate(x_refs):
        rows = x_ref.shape[0]
        out_ref[i * rows : (i + 1) * rows] = dot(x_ref[...], w_ref[...]).astype(jnp.bfloat16)


def keys_kernel(slots, *refs):
    x_refs, (wk_ref, wv_ref), (k_ref, v_ref, k_up, k_down, v_up, v_down, mixed) = (
        refs[:4],
        refs[4:6],
        refs[6:],
    )
    rows = x_refs[0].shape[0]
    whole = mixed.shape[1]
    rest = whole // 2
    mixed[:, :rest] = wk_ref[:, whole:]
    mixed[:, rest:] = wv_ref[:, whole:]
    for i, x_ref in enumerate(x_refs):
        here = slice(i * rows, (i + 1) * rows)
        k_ref[here, :whole] = dot(x_ref[...], wk_ref[:, :whole]).astype(jnp.bfloat16)
        v_ref[here, :whole] = dot(x_ref[...], wv_ref[:, :whole]).astype(jnp.bfloat16)
        found = dot(x_ref[...], mixed[...]).astype(jnp.bfloat16)
        k_ref[here, whole:] = found[:, :rest]
        v_ref[here, whole:] = found[:, rest:]
    for i in range(2):
        here = slice(i * rows, (i + 1) * rows)
        up = pl.ds(pl.multiple_of(slots[i] * rows, rows), rows)
        down = pl.ds(pl.multiple_of(slots[2 + i] * rows, rows), rows)
        k_up[here] = k_ref[up, :]
        v_up[here] = v_ref[up, :]
        k_down[here] = k_ref[down, :]
        v_down[here] = v_ref[down, :]


def queries(blocks, weights):
    rows, width = blocks[0].shape
    part = weights.shape[1]
    return pl.pallas_call(
        queries_kernel,
        out_shape=jax.ShapeDtypeStruct((4 * rows, part), jnp.bfloat16),
        in_specs=[VMEM] * 5,
        out_specs=VMEM,
        compiler_params=limit(14),
        cost_estimate=pl.CostEstimate(
            flops=8 * rows * width * part,
            bytes_accessed=2 * width * part + 8 * rows * width,
            transcendentals=0,
        ),
        name="queries",
    )(*blocks, weights)


def keys(slots, blocks, weights):
    rows, width = blocks[0].shape
    part = weights[0].shape[1]
    whole = jax.ShapeDtypeStruct((4 * rows, part), jnp.bfloat16)
    window = jax.ShapeDtypeStruct((2 * rows, part), jnp.bfloat16)
    return pl.pallas_call(
        keys_kernel,
        out_shape=[whole] * 2 + [window] * 4,
        in_specs=[SMEM] + [VMEM] * 6,
        out_specs=[VMEM] * 6,
        scratch_shapes=[pltpu.VMEM((width, 2 * part // 3), jnp.bfloat16)],
        compiler_params=limit(18),
        cost_estimate=pl.CostEstimate(
            flops=16 * rows * width * part,
            bytes_accessed=4 * width * part + 8 * rows * width,
            transcendentals=0,
        ),
        name="keys",
    )(slots, *blocks, *weights)


SCALING = HEAD_DIM ** (-0.5) * 1.4426950408889634


def weighted(scores, highest, values):
    weights = jnp.exp2((scores - highest) * SCALING).astype(jnp.bfloat16)
    return dot(weights, jnp.concatenate([values, jnp.ones_like(values)], axis=1))


def score(queries, keys):
    return lax.dot_general(
        queries, keys, (((1,), (1,)), ((), ())), preferred_element_type=jnp.float32
    )


def attend_own_kernel(q, k, v, sums, totals, peaks):
    rows = q.shape[0] // 2
    for part in range(2):
        here = slice(part * rows, (part + 1) * rows)
        scores = score(q[here], k[...])
        highest = jnp.max(scores, axis=-1, keepdims=True)
        found = weighted(scores, highest, v[...])
        sums[here] = found[:, :HEAD_DIM]
        totals[here] = found[:, HEAD_DIM:]
        peaks[here] = jnp.broadcast_to(highest, (rows, HEAD_DIM))


def attend_own(q, k, v):
    rows, width = q.shape
    full = pl.BlockSpec((rows, HEAD_DIM), lambda i: (0, i))
    return pl.pallas_call(
        attend_own_kernel,
        out_shape=[jax.ShapeDtypeStruct((rows, width), jnp.float32)] * 3,
        grid=(width // HEAD_DIM,),
        in_specs=[full] * 3,
        out_specs=[full] * 3,
        compiler_params=limit(16),
        cost_estimate=pl.CostEstimate(
            flops=4 * rows * rows * width,
            bytes_accessed=18 * rows * width,
            transcendentals=rows * rows * (width // HEAD_DIM),
        ),
        name="attend_own",
    )(q, k, v)


def attend_kernel(seen, q, sums, totals, peaks, kp, kn, k_ends, vp, vn, out0, out1):
    k_prev = jnp.where(seen[2] == 1, k_ends[...], kp[...])
    k_next = jnp.where(seen[3] == 1, k_ends[...], kn[...])
    keys = jnp.concatenate([k_prev, k_next], axis=0)
    values = jnp.concatenate([vp[...], vn[...]], axis=0)
    window = kp.shape[0]
    spot = lax.broadcasted_iota(jnp.int32, (1, 2 * window), 1)
    hidden = ((spot < window) & (seen[0] == 0)) | ((spot >= window) & (seen[1] == 0))
    shift = jnp.where(hidden, -jnp.inf, 0.0).astype(jnp.float32)
    rows = out0.shape[0]
    for part in range(2):
        here = slice(part * rows, (part + 1) * rows)
        scores = score(q[here], keys) + shift
        peak = peaks[here]
        highest = jnp.maximum(peak[:, :1], jnp.max(scores, axis=-1, keepdims=True))
        found = weighted(scores, highest, values)
        before = jnp.exp2((peak - highest) * SCALING)
        total = totals[here] * before + found[:, HEAD_DIM:]
        found = sums[here] * before + found[:, :HEAD_DIM]
        (out0, out1)[part][...] = (found / total).astype(jnp.bfloat16)


def attend(seen, q, own, kp, kn, k_ends, vp, vn):
    rows, width = q.shape
    window = kp.shape[0]
    full = pl.BlockSpec((rows, HEAD_DIM), lambda i, seen: (0, i))
    halo = pl.BlockSpec((window, HEAD_DIM), lambda i, seen: (0, i))
    out = pl.BlockSpec((rows // 2, HEAD_DIM), lambda i, seen: (0, i))
    return pl.pallas_call(
        attend_kernel,
        out_shape=[jax.ShapeDtypeStruct((rows // 2, width), jnp.bfloat16)] * 2,
        grid_spec=pltpu.PrefetchScalarGridSpec(
            num_scalar_prefetch=1,
            grid=(width // HEAD_DIM,),
            in_specs=[full] * 4 + [halo] * 5,
            out_specs=[out] * 2,
        ),
        compiler_params=limit(16),
        cost_estimate=pl.CostEstimate(
            flops=8 * rows * window * width,
            bytes_accessed=20 * rows * width,
            transcendentals=2 * rows * window * (width // HEAD_DIM),
        ),
        name="attend",
    )(seen, q, *own, kp, kn, k_ends, vp, vn)


def run_copies(pairs, sems):
    copies = [
        pltpu.make_async_copy(source, target, sems.at[i])
        for i, (source, target) in enumerate(pairs)
    ]
    for copy in copies:
        copy.start()
    for copy in copies:
        copy.wait()


def gather_kernel(along_y, w_self, w_core, *refs):
    *pieces, buffer, sems = refs
    depth = w_self.shape[0]
    tile = buffer.shape[2]
    pairs = []
    for index, columns in enumerate(tile_columns(along_y[0], tile)):
        sources = (w_self.at[:, columns], w_core.at[:, columns], pieces[index], pieces[SIDE + index])
        for i, source in enumerate(sources):
            pairs.append((source, buffer.at[index, i * depth : (i + 1) * depth]))
    run_copies(pairs, sems)


def gather_weights(along_y, w_self, *weights):
    depth, width = w_self.shape
    return pl.pallas_call(
        gather_kernel,
        out_shape=pltpu.VMEM((SIDE, 4 * depth, width // SIDE), jnp.bfloat16),
        in_specs=[SMEM] + [HBM] * 10,
        out_specs=VMEM,
        scratch_shapes=[pltpu.SemaphoreType.DMA((4 * SIDE,))],
        compiler_params=limit(4),
        cost_estimate=pl.CostEstimate(
            flops=0, bytes_accessed=16 * depth * width, transcendentals=0
        ),
        name="gather_weights",
    )(along_y, w_self, *weights)


def tile_columns(along_y, tile):
    return [
        pl.ds(pl.multiple_of(lax.rem(along_y + offset, SIDE) * tile, tile), tile)
        for offset in (0, SIDE - 1, 1, 2)
    ]


def advance_kernel(numbers, steps, *refs):
    attended, weights = refs[:4], refs[4]
    x_refs, (new_own, new_chip, gate_ref, mod_ref) = refs[5:7], refs[7:11]
    state_ref, own_ref, chip_ref, heads, held = refs[11:]
    half = own_ref.shape[0]
    depth = attended[0].shape[1]
    for i, ref in enumerate(attended):
        columns = slice(i * depth, (i + 1) * depth)
        if i < 2:
            heads[:, columns] = ref[...]
        else:
            heads[:half, columns] = ref[half:]
            heads[half:, columns] = ref[:half]
    step = steps[numbers[0]]
    fresh = numbers[1] == 1
    for index, columns in enumerate(tile_columns(numbers[2], weights.shape[2])):
        attn = dot(heads[...], weights[index])
        current = jnp.concatenate([x_ref[:, columns] for x_ref in x_refs], axis=0)
        current = current.astype(jnp.float32)
        gate = gate_ref[0, 2:3, columns]
        state = (current + step * (gate * attn - current)).astype(jnp.bfloat16)
        new = jnp.concatenate([new_own[:, columns], new_chip[:, columns]], axis=0)
        held[:, columns] = jnp.where(fresh, new, state)
    state_ref[...] = held[:half]
    normalize_rows(held.at[:half], mod_ref[0], own_ref)
    normalize_rows(held.at[half:], mod_ref[0], chip_ref)


def advance(numbers, steps, attended, weights, x_parts, new_own, new_chip, gate, modulation):
    half, width = new_own.shape
    depth = attended[0].shape[1]
    block = jax.ShapeDtypeStruct((half, width), jnp.bfloat16)
    return pl.pallas_call(
        advance_kernel,
        out_shape=[block] * 3,
        in_specs=[SMEM] * 2 + [VMEM] * 11,
        out_specs=[VMEM] * 3,
        scratch_shapes=[
            pltpu.VMEM((2 * half, 4 * depth), jnp.bfloat16),
            pltpu.VMEM((2 * half, width), jnp.bfloat16),
        ],
        compiler_params=limit(20),
        cost_estimate=pl.CostEstimate(
            flops=16 * half * depth * width,
            bytes_accessed=14 * half * width,
            transcendentals=0,
        ),
        name="advance",
    )(numbers, steps, *attended, weights, *x_parts, new_own, new_chip, gate, modulation)


def finish_kernel(numbers, steps, *refs):
    attended, (weights, first, late, ends, gate_ref, out_ref, heads) = refs[:4], refs[4:]
    depth = attended[0].shape[1]
    for i, ref in enumerate(attended):
        heads[:, i * depth : (i + 1) * depth] = ref[...]
    step = steps[numbers[0]]
    for index, columns in enumerate(tile_columns(numbers[2], weights.shape[2])):
        attn = dot(heads[...], weights[index])
        rest = jnp.where(numbers[1] == 1, ends[:, columns], late[:, columns])
        current = jnp.concatenate([first[:, columns], rest], axis=0).astype(jnp.float32)
        gate = gate_ref[0, 2:3, columns]
        out_ref[0, :, columns] = (current + step * (gate * attn - current)).astype(jnp.bfloat16)


def finish(numbers, steps, attended, weights, x_parts, gate):
    rows, depth = attended[0].shape
    width = gate.shape[2]
    return pl.pallas_call(
        finish_kernel,
        out_shape=jax.ShapeDtypeStruct((1, rows, width), jnp.bfloat16),
        in_specs=[SMEM] * 2 + [VMEM] * 9,
        out_specs=VMEM,
        scratch_shapes=[pltpu.VMEM((rows, 4 * depth), jnp.bfloat16)],
        compiler_params=limit(14),
        cost_estimate=pl.CostEstimate(
            flops=8 * rows * depth * width, bytes_accessed=4 * rows * width, transcendentals=0
        ),
        name="finish",
    )(numbers, steps, *attended, weights, *x_parts, gate)


def local(latents, new_frame, level_index, window_offsets, mod_table, step_sizes, w_qkv, w_out):
    frame = lax.axis_index("queue")
    head = lax.axis_index("head")
    along_x = lax.rem(frame, SIDE)
    along_y = frame // (SIDE * SIDE)
    rows, width = latents.shape[1:]
    part = w_qkv.shape[2]

    def head_permute(block, route):
        return lax.ppermute(block, "head", route)

    def queue_permute(block, route):
        return lax.ppermute(block, "queue", route)

    def modulation(level):
        return lax.dynamic_slice_in_dim(mod_table, level, 1, 0)

    x_own = latents[0]
    x_chip = head_permute(x_own, CHIP)
    here = jnp.concatenate([level_index, window_offsets[0]])
    after = queue_permute(here, DOWN)
    before = queue_permute(here, UP)
    second = queue_permute(here, UP_TWICE)
    quarter = width // SIDE
    share = lax.dynamic_slice_in_dim(w_out, along_y * quarter, quarter, 1)
    share = lax.ppermute(share, EVERY, ACROSS)
    w_q, w_k, w_v = (w_qkv[:, i] for i in range(3))
    after, before, w_q, w_k, w_v = lax.optimization_barrier((after, before, w_q, w_k, w_v))
    mod_first = modulation(level_index[0])
    own = norm(x_own, mod_first)
    own, share = lax.optimization_barrier((own, share))
    own_c = head_permute(own, CORE)
    w_core = head_permute(w_out, CORE)
    x_chip, own_c, w_core = lax.optimization_barrier((x_chip, own_c, w_core))
    chip = norm(x_chip, mod_first)
    chip_c = head_permute(chip, CORE)
    mod_last = modulation(before[0])

    def windows(blocks, low, high, weights):
        def slot(index):
            index = index ^ head
            return (index >> 1) | ((index & 1) << 1)

        slots = jnp.stack([slot(low), slot(low + 1), slot(high), slot(high + 1)])
        return keys(slots, blocks, weights)

    def between_rows(k_prev, k_next):
        ends = jnp.where(along_x == 0, k_prev, k_next)
        return queue_permute(ends, FIRST_UP + LAST_DOWN)

    def shown(prev, after):
        flags = (prev, after, along_x == 0, along_x == SIDE - 1)
        return jnp.stack([flag.astype(jnp.int32) for flag in flags])

    blocks = (own, chip, own_c, chip_c)
    share_low = queue_permute(share, ALONG_Y_UP)
    share_high = queue_permute(share, ALONG_Y_DOWN)
    new_chip = lax.ppermute(new_frame, EVERY, NEW_FRAME)
    k, v, k_up, k_down, v_up, v_down = windows(blocks, after[1], before[2], (w_k, w_v))
    v_prev = queue_permute(v_up, UP)
    v_next = queue_permute(v_down, DOWN)
    k_prev = queue_permute(k_up, ROW_UP)
    k_next = queue_permute(k_down, ROW_DOWN)
    k_ends = between_rows(k_prev, k_next)
    w_q_now, share_low, share_high, new_chip = lax.optimization_barrier(
        (w_q, share_low, share_high, new_chip)
    )
    q = queries(blocks, w_q_now)
    inside = attend_own(q, k, v)
    share_far = queue_permute(share_low, ALONG_Y_UP)
    seen = shown(frame > 0, frame < FRAMES - 1)
    to_same, to_other = attend(seen, q, inside, k_prev, k_next, k_ends, v_prev, v_next)
    to_same, to_other, second, w_chip = lax.optimization_barrier(
        (to_same, to_other, second, (share, share_low, share_high, share_far))
    )
    attended = (
        to_same,
        head_permute(to_other, CORE),
        head_permute(to_same, CHIP),
        head_permute(to_other, BOTH),
    )
    w_both = tuple(head_permute(piece, CORE) for piece in w_chip)
    w_rows = (w_out, w_core, *w_chip, *w_both)
    w_all = gather_weights(along_y[None], *w_rows)
    numbers = jnp.stack([here[0], (frame == 0).astype(jnp.int32), along_y])
    state, own, chip = advance(
        numbers, step_sizes, attended, w_all, (x_own, x_chip), new_frame, new_chip, mod_first, mod_last
    )

    own, chip, w_rows = lax.optimization_barrier((own, chip, w_rows))
    own_c = head_permute(own, CORE)
    chip_c = head_permute(chip, CORE)
    half = rows // 2
    x_late = queue_permute(state[half:], ROW_DOWN)
    x_first = queue_permute(state[:half], DOWN)
    blocks = (own, chip, own_c, chip_c)
    k, v, k_up, k_down, v_up, v_down = windows(blocks, here[1], second[2], (w_k, w_v))
    v_prev = queue_permute(v_up, UP)
    v_next = queue_permute(v_down, DOWN)
    k_prev = queue_permute(k_up, ROW_UP)
    k_next = queue_permute(k_down, ROW_DOWN)
    k_prev, k_next, x_first = lax.optimization_barrier((k_prev, k_next, x_first))
    k_ends = between_rows(k_prev, k_next)
    q = queries(blocks, w_q)
    inside = attend_own(q, k, v)
    inside, x_late = lax.optimization_barrier((inside, x_late))
    seen = shown(frame != 1, frame != 0)
    to_same, to_other = attend(seen, q, inside, k_prev, k_next, k_ends, v_prev, v_next)
    to_same, to_other, w_rows, x_late = lax.optimization_barrier(
        (to_same, to_other, w_rows, x_late)
    )
    x_ends = queue_permute(x_late, LAST_DOWN)
    attended = (
        lax.ppermute(to_same[:rows], EVERY, towards(-1, 0)),
        lax.ppermute(to_other[:rows], EVERY, towards(-1, 1)),
        lax.ppermute(to_same[rows:], EVERY, towards(-1, 2)),
        lax.ppermute(to_other[rows:], EVERY, towards(-1, 3)),
    )
    w_all = gather_weights(along_y[None], *w_rows)
    numbers = jnp.stack([here[0], (along_x == SIDE - 1).astype(jnp.int32), along_y])
    x_parts = (x_first, x_late, x_ends)
    return finish(numbers, step_sizes, attended, w_all, x_parts, mod_first)


def solution(mesh):
    return jax.shard_map(
        local,
        mesh=mesh,
        in_specs=(
            P("queue", "head", None),
            P("head", None),
            P("queue"),
            P("queue", None),
            P(),
            P(),
            P(None, None, "head"),
            P("head", None),
        ),
        out_specs=P("queue", "head", None),
        check_vma=False,
    )
```

```python
import functools

import jax
import jax.numpy as jnp
from jax import lax
from jax.experimental import pallas as pl
from jax.experimental.pallas import tpu as pltpu
from jax.sharding import PartitionSpec as P

HEAD_DIM = 128
EPSILON = 1e-06
MIB = 1 << 20

SIDE = 4
PLACES = [(y, z, x) for y in range(SIDE) for z in range(SIDE) for x in range(SIDE)]
FRAMES = len(PLACES)


def place(y, z, x):
    return (y % SIDE * SIDE + z % SIDE) * SIDE + x % SIDE


CORE = [(i, i ^ 1) for i in range(4)]
CHIP = [(i, i ^ 2) for i in range(4)]
BOTH = [(i, i ^ 3) for i in range(4)]
UP = [(i, (i + 1) % FRAMES) for i in range(FRAMES)]
DOWN = [(target, source) for source, target in UP]
UP_TWICE = [(i, (i + 2) % FRAMES) for i in range(FRAMES)]


def row_of(frame, x):
    return frame % FRAMES // SIDE * SIDE + x


ROW_UP = [(place(y, z, x), place(y, z, x + 1)) for y, z, x in PLACES]
ROW_DOWN = [(target, source) for source, target in ROW_UP]
FIRST_UP = [(q, row_of(q + SIDE, 0)) for q in range(FRAMES) if q % SIDE == 0]
LAST_DOWN = [(q, row_of(q - SIDE, SIDE - 1)) for q in range(FRAMES) if q % SIDE == SIDE - 1]
ACROSS = []
for y, z, x in PLACES:
    for core in range(2):
        ends = (place(y, z, x) * 4 + 2 + core, place(y, z + 1, x) * 4 + core)
        ACROSS += [ends, ends[::-1]]
ALONG_Y_UP = [(place(y, z, x), place(y + 1, z, x)) for y, z, x in PLACES]
ALONG_Y_DOWN = [(place(y, z, x), place(y - 1, z, x)) for y, z, x in PLACES]
NEW_FRAME = [
    (place(0, z, 0) * 4 + side * 2 + core, (1 - side) * 2 + core)
    for z, side in ((SIDE - 1, 1), (1, 0))
    for core in range(2)
]
EVERY = ("queue", "head")


def towards(step, mask):
    return [
        (q * 4 + h, (q + step) % FRAMES * 4 + (h ^ mask)) for q in range(FRAMES) for h in range(4)
    ]


def limit(mib):
    return pltpu.CompilerParams(vmem_limit_bytes=mib * MIB)


VMEM = pl.BlockSpec(memory_space=pltpu.VMEM)
SMEM = pl.BlockSpec(memory_space=pltpu.SMEM)
HBM = pl.BlockSpec(memory_space=pltpu.HBM)


def normalized(values, modulation):
    average = jnp.mean(values, axis=-1, keepdims=True)
    centered = values - average
    spread = jnp.mean(centered * centered, axis=-1, keepdims=True)
    return (
        centered * lax.rsqrt(spread + EPSILON) * (1.0 + modulation[1:2]) + modulation[0:1]
    ).astype(jnp.bfloat16)


def normalize_rows(x_ref, modulation, out_ref):
    chunk = 16

    def body(index, carry):
        at = pl.multiple_of(index * chunk, chunk)
        values = x_ref[pl.ds(at, chunk), :].astype(jnp.float32)
        out_ref[pl.ds(at, chunk), :] = normalized(values, modulation)
        return carry

    lax.fori_loop(0, x_ref.shape[0] // chunk, body, 0, unroll=4)


def dot(a, b):
    return jnp.dot(a, b, preferred_element_type=jnp.float32)


def norm_kernel(x_ref, mod_ref, out_ref):
    normalize_rows(x_ref, mod_ref[0], out_ref)


def norm(x, modulation):
    rows, width = x.shape
    return pl.pallas_call(
        norm_kernel,
        out_shape=jax.ShapeDtypeStruct((rows, width), jnp.bfloat16),
        in_specs=[VMEM] * 2,
        out_specs=VMEM,
        compiler_params=limit(8),
        cost_estimate=pl.CostEstimate(
            flops=10 * rows * width, bytes_accessed=4 * rows * width, transcendentals=rows
        ),
        name="norm",
    )(x, modulation)


def queries_kernel(*refs):
    *x_refs, w_ref, out_ref = refs
    for i, x_ref in enumerate(x_refs):
        rows = x_ref.shape[0]
        out_ref[i * rows : (i + 1) * rows] = dot(x_ref[...], w_ref[...]).astype(jnp.bfloat16)


def keys_kernel(slots, *refs):
    x_refs, (wk_ref, wv_ref), (k_ref, v_ref, k_up, k_down, v_up, v_down, mixed) = (
        refs[:4],
        refs[4:6],
        refs[6:],
    )
    rows = x_refs[0].shape[0]
    whole = mixed.shape[1]
    rest = whole // 2
    mixed[:, :rest] = wk_ref[:, whole:]
    mixed[:, rest:] = wv_ref[:, whole:]
    for i, x_ref in enumerate(x_refs):
        here = slice(i * rows, (i + 1) * rows)
        k_ref[here, :whole] = dot(x_ref[...], wk_ref[:, :whole]).astype(jnp.bfloat16)
        v_ref[here, :whole] = dot(x_ref[...], wv_ref[:, :whole]).astype(jnp.bfloat16)
        found = dot(x_ref[...], mixed[...]).astype(jnp.bfloat16)
        k_ref[here, whole:] = found[:, :rest]
        v_ref[here, whole:] = found[:, rest:]
    for i in range(2):
        here = slice(i * rows, (i + 1) * rows)
        up = pl.ds(pl.multiple_of(slots[i] * rows, rows), rows)
        down = pl.ds(pl.multiple_of(slots[2 + i] * rows, rows), rows)
        k_up[here] = k_ref[up, :]
        v_up[here] = v_ref[up, :]
        k_down[here] = k_ref[down, :]
        v_down[here] = v_ref[down, :]


def queries(blocks, weights):
    rows, width = blocks[0].shape
    part = weights.shape[1]
    return pl.pallas_call(
        queries_kernel,
        out_shape=jax.ShapeDtypeStruct((4 * rows, part), jnp.bfloat16),
        in_specs=[VMEM] * 5,
        out_specs=VMEM,
        compiler_params=limit(14),
        cost_estimate=pl.CostEstimate(
            flops=8 * rows * width * part,
            bytes_accessed=2 * width * part + 8 * rows * width,
            transcendentals=0,
        ),
        name="queries",
    )(*blocks, weights)


def keys(slots, blocks, weights):
    rows, width = blocks[0].shape
    part = weights[0].shape[1]
    whole = jax.ShapeDtypeStruct((4 * rows, part), jnp.bfloat16)
    window = jax.ShapeDtypeStruct((2 * rows, part), jnp.bfloat16)
    return pl.pallas_call(
        keys_kernel,
        out_shape=[whole] * 2 + [window] * 4,
        in_specs=[SMEM] + [VMEM] * 6,
        out_specs=[VMEM] * 6,
        scratch_shapes=[pltpu.VMEM((width, 2 * part // 3), jnp.bfloat16)],
        compiler_params=limit(18),
        cost_estimate=pl.CostEstimate(
            flops=16 * rows * width * part,
            bytes_accessed=4 * width * part + 8 * rows * width,
            transcendentals=0,
        ),
        name="keys",
    )(slots, *blocks, *weights)


SCALING = HEAD_DIM ** (-0.5) * 1.4426950408889634


def weighted(scores, highest, values):
    weights = jnp.exp2((scores - highest) * SCALING).astype(jnp.bfloat16)
    return dot(weights, jnp.concatenate([values, jnp.ones_like(values)], axis=1))


def score(queries, keys):
    return lax.dot_general(
        queries, keys, (((1,), (1,)), ((), ())), preferred_element_type=jnp.float32
    )


def attend_own_kernel(q, k, v, sums, totals, peaks):
    rows = q.shape[0] // 2
    for part in range(2):
        here = slice(part * rows, (part + 1) * rows)
        scores = score(q[here], k[...])
        highest = jnp.max(scores, axis=-1, keepdims=True)
        found = weighted(scores, highest, v[...])
        sums[here] = found[:, :HEAD_DIM]
        totals[here] = found[:, HEAD_DIM:]
        peaks[here] = jnp.broadcast_to(highest, (rows, HEAD_DIM))


def attend_own(q, k, v):
    rows, width = q.shape
    full = pl.BlockSpec((rows, HEAD_DIM), lambda i: (0, i))
    return pl.pallas_call(
        attend_own_kernel,
        out_shape=[jax.ShapeDtypeStruct((rows, width), jnp.float32)] * 3,
        grid=(width // HEAD_DIM,),
        in_specs=[full] * 3,
        out_specs=[full] * 3,
        compiler_params=limit(16),
        cost_estimate=pl.CostEstimate(
            flops=4 * rows * rows * width,
            bytes_accessed=18 * rows * width,
            transcendentals=rows * rows * (width // HEAD_DIM),
        ),
        name="attend_own",
    )(q, k, v)


def attend_kernel(seen, q, sums, totals, peaks, kp, kn, k_ends, vp, vn, out0, out1):
    k_prev = jnp.where(seen[2] == 1, k_ends[...], kp[...])
    k_next = jnp.where(seen[3] == 1, k_ends[...], kn[...])
    keys = jnp.concatenate([k_prev, k_next], axis=0)
    values = jnp.concatenate([vp[...], vn[...]], axis=0)
    window = kp.shape[0]
    spot = lax.broadcasted_iota(jnp.int32, (1, 2 * window), 1)
    hidden = ((spot < window) & (seen[0] == 0)) | ((spot >= window) & (seen[1] == 0))
    shift = jnp.where(hidden, -jnp.inf, 0.0).astype(jnp.float32)
    rows = out0.shape[0]
    for part in range(2):
        here = slice(part * rows, (part + 1) * rows)
        scores = score(q[here], keys) + shift
        peak = peaks[here]
        highest = jnp.maximum(peak[:, :1], jnp.max(scores, axis=-1, keepdims=True))
        found = weighted(scores, highest, values)
        before = jnp.exp2((peak - highest) * SCALING)
        total = totals[here] * before + found[:, HEAD_DIM:]
        found = sums[here] * before + found[:, :HEAD_DIM]
        (out0, out1)[part][...] = (found / total).astype(jnp.bfloat16)


def attend(seen, q, own, kp, kn, k_ends, vp, vn):
    rows, width = q.shape
    window = kp.shape[0]
    full = pl.BlockSpec((rows, HEAD_DIM), lambda i, seen: (0, i))
    halo = pl.BlockSpec((window, HEAD_DIM), lambda i, seen: (0, i))
    out = pl.BlockSpec((rows // 2, HEAD_DIM), lambda i, seen: (0, i))
    return pl.pallas_call(
        attend_kernel,
        out_shape=[jax.ShapeDtypeStruct((rows // 2, width), jnp.bfloat16)] * 2,
        grid_spec=pltpu.PrefetchScalarGridSpec(
            num_scalar_prefetch=1,
            grid=(width // HEAD_DIM,),
            in_specs=[full] * 4 + [halo] * 5,
            out_specs=[out] * 2,
        ),
        compiler_params=limit(16),
        cost_estimate=pl.CostEstimate(
            flops=8 * rows * window * width,
            bytes_accessed=20 * rows * width,
            transcendentals=2 * rows * window * (width // HEAD_DIM),
        ),
        name="attend",
    )(seen, q, *own, kp, kn, k_ends, vp, vn)


def run_copies(pairs, sems):
    copies = [
        pltpu.make_async_copy(source, target, sems.at[i])
        for i, (source, target) in enumerate(pairs)
    ]
    for copy in copies:
        copy.start()
    for copy in copies:
        copy.wait()


def gather_kernel(along_y, w_self, w_core, *refs):
    *pieces, buffer, sems = refs
    depth = w_self.shape[0]
    tile = buffer.shape[2]
    pairs = []
    for index, columns in enumerate(tile_columns(along_y[0], tile)):
        sources = (w_self.at[:, columns], w_core.at[:, columns], pieces[index], pieces[SIDE + index])
        for i, source in enumerate(sources):
            pairs.append((source, buffer.at[index, i * depth : (i + 1) * depth]))
    run_copies(pairs, sems)


def gather_weights(along_y, w_self, *weights):
    depth, width = w_self.shape
    return pl.pallas_call(
        gather_kernel,
        out_shape=pltpu.VMEM((SIDE, 4 * depth, width // SIDE), jnp.bfloat16),
        in_specs=[SMEM] + [HBM] * 10,
        out_specs=VMEM,
        scratch_shapes=[pltpu.SemaphoreType.DMA((4 * SIDE,))],
        compiler_params=limit(4),
        cost_estimate=pl.CostEstimate(
            flops=0, bytes_accessed=16 * depth * width, transcendentals=0
        ),
        name="gather_weights",
    )(along_y, w_self, *weights)


def tile_columns(along_y, tile):
    return [
        pl.ds(pl.multiple_of(lax.rem(along_y + offset, SIDE) * tile, tile), tile)
        for offset in (0, SIDE - 1, 1, 2)
    ]


def advance_kernel(numbers, steps, *refs):
    attended, weights = refs[:4], refs[4]
    x_refs, (new_own, new_chip, gate_ref, mod_ref) = refs[5:7], refs[7:11]
    state_ref, own_ref, chip_ref, heads, held = refs[11:]
    half = own_ref.shape[0]
    depth = attended[0].shape[1]
    for i, ref in enumerate(attended):
        columns = slice(i * depth, (i + 1) * depth)
        if i < 2:
            heads[:, columns] = ref[...]
        else:
            heads[:half, columns] = ref[half:]
            heads[half:, columns] = ref[:half]
    step = steps[numbers[0]]
    fresh = numbers[1] == 1
    for index, columns in enumerate(tile_columns(numbers[2], weights.shape[2])):
        attn = dot(heads[...], weights[index])
        current = jnp.concatenate([x_ref[:, columns] for x_ref in x_refs], axis=0)
        current = current.astype(jnp.float32)
        gate = gate_ref[0, 2:3, columns]
        state = (current + step * (gate * attn - current)).astype(jnp.bfloat16)
        new = jnp.concatenate([new_own[:, columns], new_chip[:, columns]], axis=0)
        held[:, columns] = jnp.where(fresh, new, state)
    state_ref[...] = held[:half]
    normalize_rows(held.at[:half], mod_ref[0], own_ref)
    normalize_rows(held.at[half:], mod_ref[0], chip_ref)


def advance(numbers, steps, attended, weights, x_parts, new_own, new_chip, gate, modulation):
    half, width = new_own.shape
    depth = attended[0].shape[1]
    block = jax.ShapeDtypeStruct((half, width), jnp.bfloat16)
    return pl.pallas_call(
        advance_kernel,
        out_shape=[block] * 3,
        in_specs=[SMEM] * 2 + [VMEM] * 11,
        out_specs=[VMEM] * 3,
        scratch_shapes=[
            pltpu.VMEM((2 * half, 4 * depth), jnp.bfloat16),
            pltpu.VMEM((2 * half, width), jnp.bfloat16),
        ],
        compiler_params=limit(20),
        cost_estimate=pl.CostEstimate(
            flops=16 * half * depth * width,
            bytes_accessed=14 * half * width,
            transcendentals=0,
        ),
        name="advance",
    )(numbers, steps, *attended, weights, *x_parts, new_own, new_chip, gate, modulation)


def finish_kernel(numbers, steps, *refs):
    attended, (weights, first, late, ends, gate_ref, out_ref, heads) = refs[:4], refs[4:]
    depth = attended[0].shape[1]
    for i, ref in enumerate(attended):
        heads[:, i * depth : (i + 1) * depth] = ref[...]
    step = steps[numbers[0]]
    for index, columns in enumerate(tile_columns(numbers[2], weights.shape[2])):
        attn = dot(heads[...], weights[index])
        rest = jnp.where(numbers[1] == 1, ends[:, columns], late[:, columns])
        current = jnp.concatenate([first[:, columns], rest], axis=0).astype(jnp.float32)
        gate = gate_ref[0, 2:3, columns]
        out_ref[0, :, columns] = (current + step * (gate * attn - current)).astype(jnp.bfloat16)


def finish(numbers, steps, attended, weights, x_parts, gate):
    rows, depth = attended[0].shape
    width = gate.shape[2]
    return pl.pallas_call(
        finish_kernel,
        out_shape=jax.ShapeDtypeStruct((1, rows, width), jnp.bfloat16),
        in_specs=[SMEM] * 2 + [VMEM] * 9,
        out_specs=VMEM,
        scratch_shapes=[pltpu.VMEM((rows, 4 * depth), jnp.bfloat16)],
        compiler_params=limit(14),
        cost_estimate=pl.CostEstimate(
            flops=8 * rows * depth * width, bytes_accessed=4 * rows * width, transcendentals=0
        ),
        name="finish",
    )(numbers, steps, *attended, weights, *x_parts, gate)


def local(latents, new_frame, level_index, window_offsets, mod_table, step_sizes, w_qkv, w_out):
    frame = lax.axis_index("queue")
    head = lax.axis_index("head")
    along_x = lax.rem(frame, SIDE)
    along_y = frame // (SIDE * SIDE)
    rows, width = latents.shape[1:]
    part = w_qkv.shape[2]

    def head_permute(block, route):
        return lax.ppermute(block, "head", route)

    def queue_permute(block, route):
        return lax.ppermute(block, "queue", route)

    def modulation(level):
        return lax.dynamic_slice_in_dim(mod_table, level, 1, 0)

    x_own = latents[0]
    x_chip = head_permute(x_own, CHIP)
    here = jnp.concatenate([level_index, window_offsets[0]])
    after = queue_permute(here, DOWN)
    before = queue_permute(here, UP)
    second = queue_permute(here, UP_TWICE)
    quarter = width // SIDE
    share = lax.dynamic_slice_in_dim(w_out, along_y * quarter, quarter, 1)
    share = lax.ppermute(share, EVERY, ACROSS)
    w_q, w_k, w_v = (w_qkv[:, i] for i in range(3))
    after, before, w_q, w_k, w_v = lax.optimization_barrier((after, before, w_q, w_k, w_v))
    mod_first = modulation(level_index[0])
    own = norm(x_own, mod_first)
    own, share = lax.optimization_barrier((own, share))
    own_c = head_permute(own, CORE)
    w_core = head_permute(w_out, CORE)
    share_c = head_permute(share, CORE)
    mod_last = modulation(before[0])

    def slots_of(low, high):
        def slot(index):
            index = index ^ head
            return (index >> 1) | ((index & 1) << 1)

        return jnp.stack([slot(low), slot(low + 1), slot(high), slot(high + 1)])

    slots = slots_of(after[1], before[2])
    x_chip, own_c, w_core, share_c, mod_last, slots = lax.optimization_barrier(
        (x_chip, own_c, w_core, share_c, mod_last, slots)
    )
    chip = norm(x_chip, mod_first)
    chip_c = head_permute(chip, CORE)

    def between_rows(k_prev, k_next):
        ends = jnp.where(along_x == 0, k_prev, k_next)
        return queue_permute(ends, FIRST_UP + LAST_DOWN)

    def shown(prev, after):
        flags = (prev, after, along_x == 0, along_x == SIDE - 1)
        return jnp.stack([flag.astype(jnp.int32) for flag in flags])

    blocks = (own, chip, own_c, chip_c)
    share_low = queue_permute(share, ALONG_Y_UP)
    share_high = queue_permute(share, ALONG_Y_DOWN)
    new_chip = lax.ppermute(new_frame, EVERY, NEW_FRAME)
    k, v, k_up, k_down, v_up, v_down = keys(slots, blocks, (w_k, w_v))
    v_prev = queue_permute(v_up, UP)
    v_next = queue_permute(v_down, DOWN)
    k_prev = queue_permute(k_up, ROW_UP)
    k_next = queue_permute(k_down, ROW_DOWN)
    k_ends = between_rows(k_prev, k_next)
    w_q_now, share_low, share_high = lax.optimization_barrier((w_q, share_low, share_high))
    q = queries(blocks, w_q_now)
    q, new_chip = lax.optimization_barrier((q, new_chip))
    inside = attend_own(q, k, v)
    share_far = queue_permute(share_low, ALONG_Y_UP)
    seen = shown(frame > 0, frame < FRAMES - 1)
    to_same, to_other = attend(seen, q, inside, k_prev, k_next, k_ends, v_prev, v_next)
    to_same, to_other, second, w_chip = lax.optimization_barrier(
        (to_same, to_other, second, (share, share_low, share_high, share_far))
    )
    attended = (
        to_same,
        head_permute(to_other, CORE),
        head_permute(to_same, CHIP),
        head_permute(to_other, BOTH),
    )
    w_both = (share_c, *(head_permute(piece, CORE) for piece in w_chip[1:]))
    w_rows = (w_out, w_core, *w_chip, *w_both)
    w_all = gather_weights(along_y[None], *w_rows)
    numbers = jnp.stack([here[0], (frame == 0).astype(jnp.int32), along_y])
    state, own, chip = advance(
        numbers, step_sizes, attended, w_all, (x_own, x_chip), new_frame, new_chip, mod_first, mod_last
    )

    own, chip, w_rows = lax.optimization_barrier((own, chip, w_rows))
    own_c = head_permute(own, CORE)
    chip_c = head_permute(chip, CORE)
    half = rows // 2
    x_late = queue_permute(state[half:], ROW_DOWN)
    x_first = queue_permute(state[:half], DOWN)
    blocks = (own, chip, own_c, chip_c)
    k, v, k_up, k_down, v_up, v_down = keys(slots_of(here[1], second[2]), blocks, (w_k, w_v))
    v_prev = queue_permute(v_up, UP)
    v_next = queue_permute(v_down, DOWN)
    k_prev = queue_permute(k_up, ROW_UP)
    k_next = queue_permute(k_down, ROW_DOWN)
    k_prev, k_next, x_first = lax.optimization_barrier((k_prev, k_next, x_first))
    k_ends = between_rows(k_prev, k_next)
    q = queries(blocks, w_q)
    inside = attend_own(q, k, v)
    inside, x_late = lax.optimization_barrier((inside, x_late))
    seen = shown(frame != 1, frame != 0)
    to_same, to_other = attend(seen, q, inside, k_prev, k_next, k_ends, v_prev, v_next)
    to_same, to_other, w_rows, x_late = lax.optimization_barrier(
        (to_same, to_other, w_rows, x_late)
    )
    x_ends = queue_permute(x_late, LAST_DOWN)
    attended = (
        lax.ppermute(to_same[:rows], EVERY, towards(-1, 0)),
        lax.ppermute(to_other[:rows], EVERY, towards(-1, 1)),
        lax.ppermute(to_same[rows:], EVERY, towards(-1, 2)),
        lax.ppermute(to_other[rows:], EVERY, towards(-1, 3)),
    )
    w_all = gather_weights(along_y[None], *w_rows)
    numbers = jnp.stack([here[0], (along_x == SIDE - 1).astype(jnp.int32), along_y])
    x_parts = (x_first, x_late, x_ends)
    return finish(numbers, step_sizes, attended, w_all, x_parts, mod_first)


def solution(mesh):
    return jax.shard_map(
        local,
        mesh=mesh,
        in_specs=(
            P("queue", "head", None),
            P("head", None),
            P("queue"),
            P("queue", None),
            P(),
            P(),
            P(None, None, "head"),
            P("head", None),
        ),
        out_specs=P("queue", "head", None),
        check_vma=False,
    )
```
